32 devices in a mesh: replica: 2 (over x), tenant: 16 (over z, y, core).
Axes of the slice: x: 2, y: 2, z: 4, core: 2. Of those that a mesh axis runs over, the one named last changes fastest.
Arguments:
- prefill_rows: bfloat16 [8192, 8192], P(('replica', 'tenant')), parts along dimension 0, may hold values from -6 to 6
- tenant_ids: int32 [8192, 1], P(('replica', 'tenant')), parts along dimension 0, may hold values from 0 to 31; in each aligned block of 256 rows (0 to 255, 256 to 511, ...) at most 16 rows name the same one
- owner_slot: int32 [32], replicated, may hold values from 0 to 31, each once
- decode_rows: bfloat16 [256, 8192], P(('replica', 'tenant')), parts along dimension 0, may hold values from -6 to 6
- queries: bfloat16 [256, 4096], P(('replica', 'tenant')), parts along dimension 0
- key_store_cache: bfloat16 [256, 384, 512], P(('replica', 'tenant')), parts along dimension 0
- value_store_cache: bfloat16 [256, 384, 512], P(('replica', 'tenant')), parts along dimension 0, may hold values from -6 to 6
- context_len: int32 [256], P(('replica', 'tenant')), parts along dimension 0, may hold values from 96 to 384, as said below
- base_weight: bfloat16 [8192, 1024], P('tenant'), may hold values from -0.0625 to 0.0625
- adapter_down: bfloat16 [32, 32, 8192], P('tenant'), may hold values from -0.0625 to 0.0625
- adapter_up: bfloat16 [32, 32, 1024], P('tenant'), may hold values from -1 to 1
Outputs:
- projected: bfloat16 [8192, 1024], P(('replica', 'tenant')), parts along dimension 0
- attended: bfloat16 [256, 4096], P(('replica', 'tenant')), parts along dimension 0
The draws below stay inside these ranges and needn't reach their ends.
There are 2 independent parts, one for each index of `replica`. The reference program is written for one: setup_inputs(seed, part) draws one part's arguments, and reference() takes and returns one part's arrays. A program takes and returns all parts, laid end to end along the dimension named above; an argument that names none is the same for every part. Nothing has to cross between parts.
Inputs may be any that keep to these rules, and one draw needn't show every extreme that they name: `tenant_ids`: the rows of one device name one tenant at most 16 times, and in some device some tenant exactly 16 times. `owner_slot`: each slot is named once. `context_len`: the first decode row of each part has 384.
All inputs are finite; a program needn't handle non-finite values.
Results may differ from the reference program's by a relative error of at most 0.0055.
Values may be sent and summed in bfloat16 or wider, within the bound.
No kernel may reach another device: no remote copies, remote signals or barrier semaphores. Data moves between devices by JAX's collectives and lax.ppermute only.
A program may use at most 128 MiB of HBM per device.

```python
import math
import jax
import jax.numpy as jnp
import numpy as np
from jax import lax

D = 8192
QUERY_HEADS = 32
KEY_VALUE_HEADS = 4
HEAD_SIZE = 128
RANK = 32
ROWS_DEV = 256
CONTEXT_SPAN = 384
KEY_WIDTH = 512
TENANTS = 32
CAP = 16
ROWS = 4096
DECODE_TOTAL = 128


def shared_keys(key):
    drawn_projection = jax.random.normal(jax.random.fold_in(key, 101), (DECODE_TOTAL, CONTEXT_SPAN, KEY_WIDTH), jnp.float32)
    return drawn_projection


def draw_key_store_cache(key, part):
    drawn_projection = shared_keys(key)
    return drawn_projection.astype(jnp.bfloat16)


def draw_queries(key, part):
    key = jax.random.fold_in(key, 9)
    values = jax.random.normal(key, (DECODE_TOTAL, QUERY_HEADS * HEAD_SIZE), jnp.float32)
    return values.astype(jnp.bfloat16)


def draw_context_len(key, part):
    key = jax.random.fold_in(key, 5)
    lengths = jax.random.randint(key, (DECODE_TOTAL,), CONTEXT_SPAN // 4, CONTEXT_SPAN + 1, dtype=jnp.int32)
    return lengths.at[0].set(CONTEXT_SPAN)


def levels(rng, extent, cuts, smallest, high):
    def one(position, shards_of):
        steps = jax.random.uniform(jax.random.fold_in(jax.random.fold_in(rng, 6), position), (shards_of,), jnp.float32, smallest / len(cuts), high / len(cuts))
        return jnp.repeat(jnp.exp(steps), extent[position] // shards_of).reshape((-1,) + (1,) * (len(extent) - position - 1))

    loudness = one(*cuts[0])
    for cut in cuts[1:]:
        loudness = loudness * one(*cut)
    return loudness


def routed_block(key, own, number, rows, count, top, bound, lean):
    sequence = jax.random.permutation(key, count)
    heavy_load, ordinary = portions_of(count, rows * top, bound, lean, True), portions_of(count, rows * top, bound, lean, False)
    places = jnp.arange(count)

    def named(sizes, turn):
        used = int((sizes > 0).sum())
        fixed = max(1, used // 4)
        moved = fixed + (places - fixed + turn * (used - fixed)) % max(1, count - fixed)
        return jnp.zeros((count,), jnp.int32).at[sequence[jnp.where(places < fixed, places, moved)]].set(jnp.asarray(sizes, jnp.int32))

    sizes = jnp.where(number % 4 == 0, named(heavy_load, number // 4), named(ordinary, number - number // 4 - 1))
    mixed = jax.random.permutation(jax.random.fold_in(own, 3), count)
    giver, sink = mixed[0:count // 2 * 2:2], mixed[1:count // 2 * 2:2]
    slack = jnp.minimum(sizes[giver] - 1, bound - sizes[sink]) // 2
    slack = jnp.where((giver == sequence[0]) | (sink == sequence[0]) | (sizes[sink] == 0), 0, jnp.maximum(slack, 0))
    moved = jax.random.randint(jax.random.fold_in(own, 4), (count // 2,), 0, 1 << 20) % (slack + 1)
    sizes = sizes.at[giver].add(-moved).at[sink].add(moved)
    labels = jnp.searchsorted(jnp.cumsum(sizes), jnp.arange(rows * top), side="right").astype(jnp.int32)
    listing = labels.reshape(top, rows).T
    listing = listing[jax.random.permutation(jax.random.fold_in(own, 1), rows)]
    turn = jax.random.randint(jax.random.fold_in(own, 2), (rows, 1), 0, top)
    return jnp.take_along_axis(listing, (jnp.arange(top)[None, :] + turn) % top, axis=1)


def portions_of(number_of, total, bound, slope, full):
    weights = [(1 << 20) // math.isqrt(grade ** slope) + 1 for grade in range(1, number_of + 1)]
    largest = bound if full else min(bound, max(-(-total // number_of), total * weights[0] // sum(weights)))
    least = 1 if total - largest >= number_of - 1 else 0
    given, spare = [largest] + [least] * (number_of - 1), total - largest - least * (number_of - 1)
    while spare > 0:
        free = [i for i in range(1, number_of) if given[i] < largest] or [i for i in range(1, number_of) if given[i] < bound]
        mass, remaining = sum([weights[i] for i in free]), spare
        for i in free:
            more = min(bound - given[i], max(1, remaining * weights[i] // mass), spare)
            given[i] = given[i] + more
            spare = spare - more
    return np.array(given)


def bell_draw(own_key, shape, spread, most, cuts=(), held_as=jnp.bfloat16):
    entries = jax.random.normal(own_key, shape, jnp.float32) * spread
    if len(cuts) > 0:
        entries = levels(own_key, shape, cuts, -0.22, 0.18) * entries
    return jnp.clip(entries, min=-most, max=most).astype(held_as)


def setup_inputs(seed: int = 0, part: int = 0) -> dict:
    key_list = jax.random.split(jax.random.key(seed), 12)
    own_keys = jax.random.split(jax.random.fold_in(key_list[11], part), 12)
    prefill_rows = bell_draw(own_keys[0], (ROWS, D), 1.0, 6.0, ((0, 16),))
    tenant_ids_keys = jax.random.split(jax.random.fold_in(own_keys[1], 1), ROWS // ROWS_DEV)
    tenant_ids_turns = jax.random.permutation(jax.random.fold_in(own_keys[1], 3), ROWS // ROWS_DEV)
    tenant_ids = jax.vmap(lambda own, number: routed_block(jax.random.fold_in(own_keys[1], 2), own, number, ROWS_DEV, TENANTS, 1, CAP, 2))(tenant_ids_keys, tenant_ids_turns).reshape((ROWS, 1))
    owner_slot = jax.random.permutation(key_list[2], TENANTS).astype(jnp.int32)
    decode_rows = bell_draw(own_keys[3], (DECODE_TOTAL, D), 1.0, 6.0, ((0, 16),))
    queries = draw_queries(jax.random.fold_in(jax.random.fold_in(key_list[11], part), 71), part)
    key_store_cache = draw_key_store_cache(jax.random.fold_in(jax.random.fold_in(key_list[11], part), 71), part)
    value_store_cache = bell_draw(own_keys[6], (DECODE_TOTAL, CONTEXT_SPAN, KEY_WIDTH), 1.0, 6.0, ((0, 16),))
    context_len = draw_context_len(jax.random.fold_in(jax.random.fold_in(key_list[11], part), 71), part)
    base_weight = bell_draw(key_list[8], (D, 2 * KEY_WIDTH), D ** -0.5, 0.0625, ((0, 16),))
    adapter_down = bell_draw(key_list[9], (TENANTS, RANK, D), D ** -0.5, 0.0625, ((0, 16),))
    adapter_up = bell_draw(key_list[10], (TENANTS, RANK, 2 * KEY_WIDTH), RANK ** -0.5, 1.0, ((0, 16),))
    return dict(prefill_rows=prefill_rows, tenant_ids=tenant_ids, owner_slot=owner_slot, decode_rows=decode_rows, queries=queries, key_store_cache=key_store_cache, value_store_cache=value_store_cache, context_len=context_len, base_weight=base_weight, adapter_down=adapter_down, adapter_up=adapter_up)


adapter_scale = 2.0

def reference(prefill_rows, tenant_ids, owner_slot, decode_rows, queries, key_store_cache, value_store_cache, context_len, base_weight, adapter_down, adapter_up):
    plain_projection = jnp.dot(prefill_rows, base_weight, preferred_element_type=jnp.float32)
    slots = owner_slot[tenant_ids[:, 0]].astype(jnp.int32)
    block = math.gcd(ROWS, 64)

    def adapt_block(pair):
        rows_block, slots_block = pair
        down = adapter_down[slots_block].astype(jnp.float32)
        lowered = jnp.einsum('bd,brd->br', rows_block.astype(jnp.float32), down).astype(jnp.bfloat16)
        upper = adapter_up[slots_block].astype(jnp.float32)
        return jnp.einsum('br,bre->be', lowered.astype(jnp.float32), upper).astype(jnp.bfloat16)
    adapter_updates = lax.map(adapt_block, (prefill_rows.reshape(ROWS // block, block, D), slots.reshape(ROWS // block, block)))
    adapter_updates = adapter_updates.reshape(ROWS, 2 * KEY_WIDTH)
    projected = (plain_projection + adapter_scale * adapter_updates.astype(jnp.float32)).astype(jnp.bfloat16)
    recent_output = jnp.dot(decode_rows, base_weight, preferred_element_type=jnp.float32).astype(jnp.bfloat16)
    query_groups = QUERY_HEADS // KEY_VALUE_HEADS
    newest_keys = recent_output[:, :KEY_WIDTH].reshape(DECODE_TOTAL, KEY_VALUE_HEADS, HEAD_SIZE).astype(jnp.float32)
    newest_values = recent_output[:, KEY_WIDTH:].reshape(DECODE_TOTAL, KEY_VALUE_HEADS, HEAD_SIZE).astype(jnp.float32)
    query_head_rows = queries.reshape(DECODE_TOTAL, KEY_VALUE_HEADS, query_groups, HEAD_SIZE).astype(jnp.float32)
    stored_keys = key_store_cache.reshape(DECODE_TOTAL, CONTEXT_SPAN, KEY_VALUE_HEADS, HEAD_SIZE).astype(jnp.float32)
    stored_values = value_store_cache.reshape(DECODE_TOTAL, CONTEXT_SPAN, KEY_VALUE_HEADS, HEAD_SIZE).astype(jnp.float32)
    reverse_permute = 1.0 / math.sqrt(HEAD_SIZE)
    scores = jnp.einsum('bkgd,bckd->bkgc', query_head_rows, stored_keys) * reverse_permute
    tenant_local = jnp.einsum('lemx,lex->lem', query_head_rows, newest_keys) * reverse_permute
    live = jnp.arange(CONTEXT_SPAN, dtype=jnp.int32)[None, :] < context_len[:, None]
    scores = jnp.where(live[:, None, None, :], scores, -jnp.inf)
    top = jnp.maximum(lax.optimization_barrier(jnp.max(scores, axis=-1)), tenant_local)
    cached_weight = jnp.exp(scores - top[..., None])
    own_weight = jnp.exp(tenant_local - top)
    total = lax.optimization_barrier(jnp.sum(cached_weight, axis=-1)) + own_weight
    probs = (cached_weight / total[..., None]).astype(jnp.bfloat16)
    probs_own = (own_weight / total).astype(jnp.bfloat16)
    mixed = jnp.einsum('bkgc,bckd->bkgd', probs.astype(jnp.float32), stored_values)
    mixed = mixed + probs_own.astype(jnp.float32)[..., None] * newest_values[:, :, None, :]
    attended = mixed.reshape(DECODE_TOTAL, QUERY_HEADS * HEAD_SIZE).astype(jnp.bfloat16)
    return (projected, attended)
```

```python
import math

import jax
import jax.numpy as jnp
from jax import lax
from jax.experimental import pallas as pl
from jax.experimental.pallas import tpu as pltpu
from jax.sharding import PartitionSpec as P

HEAD_SIZE = 128
adapter_scale = 2.0
BOTH = ("replica", "tenant")


def cost(flops, bytes_accessed):
    return pl.CostEstimate(flops=flops, bytes_accessed=bytes_accessed, transcendentals=0)


def split_columns(prefill, decode, slots_row, down, up, base, table, steps, kk, flips, rep):
    rows, dec = prefill.shape[0], decode.shape[0]
    pad = slots_row.shape[0]
    ranks = down.shape[0]
    wide = steps * kk
    out_width = up.shape[1]
    fold = wide // out_width
    tall = ranks // fold
    if kk % 128:
        stacked = jnp.concatenate([prefill, decode], axis=0)

        def pick(a, m):
            cut = a.reshape(a.shape[0], -1, kk)
            return jnp.take(cut, table[m * steps : (m + 1) * steps], axis=1).reshape(a.shape[0], wide)

        folded = jnp.concatenate(jnp.split(up, fold, axis=0), axis=1)
        return (
            [jnp.concatenate([pick(stacked, m), slots_row], axis=0) for m in range(4)],
            [jnp.concatenate([pick(down, m), folded], axis=0) for m in flips],
            lax.dynamic_slice_in_dim(base, rep * kk, kk, axis=0),
        )
    count = len(flips)
    per = out_width // kk

    def kernel(tab, *refs):
        pre, dcd, dwn = refs[0:4], refs[4:8], refs[8 : 8 + count]
        slot, upm, bas = refs[8 + count : 11 + count]
        outs = refs[11 + count :]
        for m in range(4):
            outs[m][0:rows, :] = pre[m][...]
            outs[m][rows : rows + dec + pad, :] = jnp.concatenate([dcd[m][...], slot[...]], axis=0)
        for i in range(count):
            outs[4 + i][0:ranks, :] = dwn[i][...]
            outs[4 + i][ranks : ranks + tall, :] = upm[...]
        outs[4 + count][...] = bas[...]

    def at(m):
        return lambda j, tab: (0, tab[m * steps + j])

    here = lambda j, tab: (0, j)
    base_rows = kk // steps
    outs = pl.pallas_call(
        kernel,
        grid_spec=pltpu.PrefetchScalarGridSpec(
            num_scalar_prefetch=1,
            grid=(steps,),
            in_specs=[pl.BlockSpec((rows, kk), at(m)) for m in range(4)]
            + [pl.BlockSpec((dec, kk), at(m)) for m in range(4)]
            + [pl.BlockSpec((ranks, kk), at(m)) for m in flips]
            + [
                pl.BlockSpec((pad, kk), here),
                pl.BlockSpec((tall, kk), lambda j, tab: (j // per, j % per)),
                pl.BlockSpec((base_rows, out_width), lambda j, tab: (tab[4 * steps] * steps + j, 0)),
            ],
            out_specs=[pl.BlockSpec((rows + dec + pad, kk), here)] * 4
            + [pl.BlockSpec((ranks + tall, kk), here)] * count
            + [pl.BlockSpec((base_rows, out_width), lambda j, tab: (j, 0))],
        ),
        out_shape=[jax.ShapeDtypeStruct((rows + dec + pad, wide), jnp.bfloat16)] * 4
        + [jax.ShapeDtypeStruct((ranks + tall, wide), jnp.bfloat16)] * count
        + [jax.ShapeDtypeStruct((kk, out_width), jnp.bfloat16)],
        compiler_params=pltpu.CompilerParams(vmem_limit_bytes=32 * 2**20),
        cost_estimate=cost(0, 10 * 2**20),
        name="split_columns",
    )(table, *([prefill] * 4), *([decode] * 4), *([down] * count), slots_row, up, base)
    return list(outs[:4]), list(outs[4 : 4 + count]), outs[4 + count]


def base_products(blocks, parts, spots, kinds):
    kk, out_width = parts[0].shape
    tall = blocks[0].shape[0]
    n = len(parts)
    if kk % 128:
        quarter = jnp.zeros((n * kk, out_width), jnp.bfloat16)
        for i in range(n):
            quarter = lax.dynamic_update_slice_in_dim(quarter, parts[i], spots[i] * kk, axis=0)
        return [
            jnp.dot(b, quarter, preferred_element_type=jnp.float32).astype(kind)
            for b, kind in zip(blocks, kinds)
        ]
    count = len(blocks)
    cut = 256

    def kernel(spot, *refs):
        rows, weights, outs = refs[:count], refs[count : count + n], refs[count + n :]
        for m in range(count):
            total = None
            for i in range(n):
                columns = pl.ds(pl.multiple_of(spot[i] * kk, kk), kk)
                term = jnp.dot(
                    rows[m][:, columns], weights[i][...], preferred_element_type=jnp.float32
                )
                total = term if total is None else total + term
            outs[m][...] = total.astype(kinds[m])

    return pl.pallas_call(
        kernel,
        grid_spec=pltpu.PrefetchScalarGridSpec(
            num_scalar_prefetch=1,
            grid=(out_width // cut,),
            in_specs=[pl.BlockSpec(blocks[0].shape, lambda j, s: (0, 0))] * count
            + [pl.BlockSpec((kk, cut), lambda j, s: (0, j))] * n,
            out_specs=[pl.BlockSpec((tall, cut), lambda j, s: (0, j))] * count,
        ),
        out_shape=[jax.ShapeDtypeStruct((tall, out_width), kind) for kind in kinds],
        compiler_params=pltpu.CompilerParams(vmem_limit_bytes=40 * 2**20),
        cost_estimate=cost(2 * count * tall * n * kk * out_width, (count * tall + out_width) * 2 * n * kk),
        name="base_products",
    )(spots, *blocks, *parts)


def lowered_products(blocks, pieces, columns, rows, first, ranks, earlier):
    wide = blocks[0].shape[1]
    total_ranks = len(pieces) * ranks
    count = len(blocks)
    if wide % 512 or columns.shape[1] * len(blocks) > 8192:
        sums = []
        down = jnp.concatenate([p[:ranks] for p in pieces], axis=0)
        for m, b in enumerate(blocks):
            product = lax.dot_general(
                b[:rows], down, (((1,), (1,)), ((), ())), preferred_element_type=jnp.float32
            )
            slot = b[first, :rows].astype(jnp.float32)
            kept = jnp.where(slot[:, None] == columns[:1], product, 0.0)
            kept = sum(kept[:, i : i + 128] for i in range(0, total_ranks, 128))
            sums.append(kept if earlier is None else earlier[m] + kept)
        return sums
    chunk = 512
    chunks = wide // chunk
    n = len(pieces)
    base_row = first // 16 * 16

    def kernel(*refs):
        xs, ds = refs[:count], refs[count : count + n]
        col = refs[count + n]
        before = refs[count + n + 1 : count + n + 1 + (0 if earlier is None else count)]
        outs = refs[count + n + 1 + len(before) : -2]
        acc, slot_of = refs[-2], refs[-1]
        j = pl.program_id(0)

        @pl.when(j == 0)
        def _():
            acc[...] = jnp.zeros_like(acc)
            for m in range(count):
                slot_of[m] = xs[m][base_row : base_row + 16, :rows].astype(jnp.float32)

        down = jnp.concatenate([d[...] for d in ds], axis=0)
        for m in range(count):
            acc[m] += lax.dot_general(
                xs[m][:rows], down, (((1,), (1,)), ((), ())), preferred_element_type=jnp.float32
            )

        @pl.when(j == chunks - 1)
        def _():
            for m in range(count):
                slot = jnp.transpose(slot_of[m])[:, first - base_row : first - base_row + 1]
                kept = None
                for i in range(0, total_ranks, 128):
                    part = jnp.where(slot == col[0:1, i : i + 128], acc[m, :, i : i + 128], 0.0)
                    kept = part if kept is None else kept + part
                outs[m][...] = kept if earlier is None else kept + before[m][...]

    whole = lambda j: (0, 0)
    extra = [] if earlier is None else list(earlier)
    return pl.pallas_call(
        kernel,
        grid=(chunks,),
        in_specs=[pl.BlockSpec((blocks[0].shape[0], chunk), lambda j: (0, j))] * count
        + [pl.BlockSpec((ranks, chunk), lambda j: (0, j))] * n
        + [pl.BlockSpec(columns.shape, whole)]
        + [pl.BlockSpec((rows, 128), whole)] * len(extra),
        out_specs=[pl.BlockSpec((rows, 128), whole)] * count,
        out_shape=[jax.ShapeDtypeStruct((rows, 128), jnp.float32)] * count,
        scratch_shapes=[
            pltpu.VMEM((count, rows, total_ranks), jnp.float32),
            pltpu.VMEM((count, 16, rows), jnp.float32),
        ],
        compiler_params=pltpu.CompilerParams(vmem_limit_bytes=40 * 2**20),
        cost_estimate=cost(2 * count * rows * wide * total_ranks, (count * rows + total_ranks) * 2 * wide),
        name="lowered_products",
    )(*blocks, *pieces, columns, *extra)


def finish(parts, block, pieces, columns, base, rows, first, ranks, rank):
    packed_rows = parts[0].shape[0]
    folds = rows // packed_rows
    tall = pieces[0].shape[0] - ranks
    out_width = base.shape[1]
    fold = ranks // tall
    n = len(pieces)
    base_row = first // 16 * 16
    if n > 16:
        lowered = sum(parts[1:], parts[0]).astype(jnp.bfloat16)
        lowered = jnp.concatenate(
            [lowered[:, b * rank : (b + 1) * rank] for b in range(folds)], axis=0
        )
        up = jnp.concatenate(
            [p[ranks:, i * out_width : (i + 1) * out_width] for p in pieces for i in range(fold)], axis=0
        )
        slot = block[first, :rows].astype(jnp.float32)
        spread = jnp.where(
            slot[:, None] == columns[:1], jnp.tile(lowered, (1, n * ranks // rank)), jnp.bfloat16(0)
        )
        delta = jnp.dot(spread, up, preferred_element_type=jnp.float32).astype(jnp.bfloat16)
        return (base[:rows] + adapter_scale * delta.astype(jnp.float32)).astype(jnp.bfloat16)

    def kernel(*refs):
        packs = refs[:4]
        blk, col, bas = refs[4:7]
        ups = refs[7 : 7 + n]
        out = refs[7 + n]
        slot = jnp.transpose(blk[...].astype(jnp.float32))[:, first - base_row : first - base_row + 1]
        packed = (packs[0][...] + packs[1][...]) + (packs[2][...] + packs[3][...])
        lane = lax.broadcasted_iota(jnp.int32, packed.shape, 1) // rank
        spread = []
        for b in range(folds):
            one = jnp.where(lane == b, packed, 0.0)
            one = one + pltpu.roll(one, rank, 1)
            one = one + pltpu.roll(one, 2 * rank, 1)
            spread.append(one)
        lowered = jnp.concatenate(spread, axis=0)
        wide = []
        for i in range(0, n * ranks, 128):
            wide.append(jnp.where(slot == col[0:1, i : i + 128], lowered, 0.0).astype(jnp.bfloat16))
        wide = jnp.concatenate(wide, axis=1)
        up = jnp.concatenate(
            [p[:, i * out_width : (i + 1) * out_width] for p in ups for i in range(fold)], axis=0
        )
        for i in range(0, out_width, 256):
            delta = jnp.dot(wide, up[:, i : i + 256], preferred_element_type=jnp.float32)
            delta = delta.astype(jnp.bfloat16).astype(jnp.float32)
            out[:, i : i + 256] = (bas[0:rows, i : i + 256] + adapter_scale * delta).astype(jnp.bfloat16)

    one = lambda j: (0, 0)
    return pl.pallas_call(
        kernel,
        grid=(1,),
        in_specs=[pl.BlockSpec(parts[0].shape, one)] * 4
        + [
            pl.BlockSpec((16, rows), lambda j: (base_row // 16, 0)),
            pl.BlockSpec(columns.shape, one),
            pl.BlockSpec(base.shape, one),
        ]
        + [pl.BlockSpec((tall, pieces[0].shape[1]), lambda j: (ranks // tall, 0))] * n,
        out_specs=pl.BlockSpec((rows, out_width), one),
        out_shape=jax.ShapeDtypeStruct((rows, out_width), jnp.bfloat16),
        compiler_params=pltpu.CompilerParams(vmem_limit_bytes=40 * 2**20),
        cost_estimate=cost(2 * rows * n * ranks * out_width, 4 * 2**20),
        name="finish",
    )(*parts, block, columns, base, *pieces)


def body(
    prefill_rows,
    tenant_ids,
    owner_slot,
    decode_rows,
    queries,
    key_store_cache,
    value_store_cache,
    context_len,
    base_weight,
    adapter_down,
    adapter_up,
):
    reps, peers = lax.axis_size("replica"), lax.axis_size("tenant")
    planes = reps * peers // 8
    sides = peers // (2 * planes)
    local_slots, rank, width = adapter_down.shape
    slots_all = local_slots * peers
    rows, dec = prefill_rows.shape[0], decode_rows.shape[0]
    out_width = base_weight.shape[1]
    half_width = out_width // 2
    kk = base_weight.shape[0] // reps
    steps = 2 * planes
    quarter = steps * kk
    pad = 16 - dec % 16
    r, t = lax.axis_index("replica"), lax.axis_index("tenant")
    z, y, c = t // (2 * sides), (t // 2) % sides, t % 2
    q = y * reps + r

    order = list(range(0, planes, 2)) + list(range(1, planes, 2))[::-1]
    after = {order[i]: order[(i + 1) % planes] for i in range(planes)}
    everyone = [(a, b) for a in range(reps) for b in range(peers)]

    def flip(m):
        pairs = []
        for a, b in everyone:
            other = (((b // 2) % sides) * reps + a) ^ m
            to = (b // (2 * sides) * sides + other // reps) * 2 + b % 2
            pairs.append((a * peers + b, (other % reps) * peers + to))
        return pairs

    flips = {m: flip(m) for m in (1, 2, 3)}
    ring = [
        (a * peers + b, a * peers + after[b // (2 * sides)] * 2 * sides + b % (2 * sides))
        for a, b in everyone
    ]
    cores = [(a * peers + b, a * peers + (b ^ 1)) for a, b in everyone]

    def send(value, pairs):
        return lax.ppermute(value, BOTH, pairs)

    place = jnp.where(z % 2 == 0, z // 2, planes - 1 - z // 2)

    def plane_of(k):
        spot = (place - k + planes) % planes
        return jnp.where(spot < planes // 2, 2 * spot, 2 * (planes - 1 - spot) + 1)

    j = jnp.arange(steps, dtype=jnp.int32)[None, :]
    other = q ^ jnp.arange(4, dtype=jnp.int32)[:, None]
    shard = (j // 2 * sides + other // reps) * 2 + j % 2
    table = jnp.concatenate([(shard * reps + other % reps).reshape(-1), r[None]])
    spots = plane_of(j[0] // 2) * 2 + (c ^ (j[0] % 2))

    tenant_hot = tenant_ids == jnp.arange(slots_all, dtype=jnp.int32)[None, :]
    slot_index = jnp.sum(jnp.where(tenant_hot, owner_slot[None, :], 0), axis=1)
    slots_row = jnp.broadcast_to(
        jnp.pad(slot_index.astype(jnp.bfloat16), (0, quarter - rows))[None, :], (pad, quarter)
    )
    ranks = local_slots * rank
    y_flips = [0, reps] if sides == 2 else [0]
    messages, adapters, held = split_columns(
        prefill_rows,
        decode_rows,
        slots_row,
        adapter_down.reshape(ranks, width),
        adapter_up.reshape(ranks, out_width),
        base_weight,
        table,
        steps,
        kk,
        y_flips,
        r,
    )
    blocks = [messages[0]] + [send(messages[m], flips[m]) for m in (1, 2, 3)]

    base_parts = []
    for k in range(planes):
        base_parts += [held, send(held, cores)]
        if k + 1 < planes:
            held = send(held, ring)

    chains = [adapters[0]] + [send(a, flips[reps]) for a in adapters[1:]]
    pieces = []
    for k in range(planes):
        pieces.append(chains + [send(a, cores) for a in chains])
        if k + 1 < planes:
            chains = [send(a, ring) for a in chains]

    sent = base_products(blocks[1:], base_parts, spots, [jnp.bfloat16] * 3)
    sent = [send(sent[m - 1], flips[m]) for m in (1, 2, 3)]
    (base,) = base_products(blocks[:1], base_parts, spots, [jnp.float32])
    base = base + sum(s.astype(jnp.float32) for s in sent)
    recent_output = base[rows : rows + dec].astype(jnp.bfloat16)

    group = jnp.arange(slots_all, dtype=jnp.int32)
    inner = group % local_slots
    side = (group // local_slots) % sides
    core = (group // (local_slots * sides)) % 2
    step = group // (local_slots * sides * 2)
    column_slot = ((plane_of(step) * sides + (y ^ side)) * 2 + (c ^ core)) * local_slots + inner
    columns = jnp.broadcast_to(
        jnp.repeat(column_slot, rank).astype(jnp.float32)[None, :], (8, slots_all * rank)
    )
    front = sum(pieces[:-1], [])
    cut = len(front) * ranks
    first = rows + dec
    sums = None
    if front:
        sums = lowered_products(blocks, front, columns[:, :cut], rows, first, ranks, None)
    sums = lowered_products(blocks, pieces[-1], columns[:, cut:], rows, first, ranks, sums)
    folds = 128 // rank
    packed = []
    for s in sums:
        s = sum(s[:, i * rank : (i + 1) * rank] for i in range(folds))
        packed.append(jnp.concatenate(jnp.split(s, folds, axis=0), axis=1))
    packed = [packed[0]] + [send(packed[m], flips[m]) for m in (1, 2, 3)]
    projected = finish(
        packed, blocks[0], sum(pieces, []), columns, base, rows, first, ranks, rank
    )

    kv_heads = half_width // HEAD_SIZE
    query_groups = queries.shape[1] // half_width
    positions = key_store_cache.shape[1]
    newest_keys = recent_output[:, :half_width].reshape(dec, kv_heads, HEAD_SIZE)
    newest_values = recent_output[:, half_width:].reshape(dec, kv_heads, HEAD_SIZE)
    query_head_rows = queries.reshape(dec, kv_heads, query_groups, HEAD_SIZE)
    stored_keys = key_store_cache.reshape(dec, positions, kv_heads, HEAD_SIZE)
    stored_values = value_store_cache.reshape(dec, positions, kv_heads, HEAD_SIZE)
    scale = 1.0 / math.sqrt(HEAD_SIZE)
    scores = (
        jnp.einsum(
            "bkgd,bckd->bkgc", query_head_rows, stored_keys, preferred_element_type=jnp.float32
        )
        * scale
    )
    own_score = (
        jnp.einsum(
            "bkgd,bkd->bkg", query_head_rows, newest_keys, preferred_element_type=jnp.float32
        )
        * scale
    )
    live = jnp.arange(positions, dtype=jnp.int32)[None, :] < context_len[:, None]
    scores = jnp.where(live[:, None, None, :], scores, -jnp.inf)
    top = jnp.maximum(jnp.max(scores, axis=-1), own_score)
    cached_weight = jnp.exp(scores - top[..., None])
    own_weight = jnp.exp(own_score - top)
    total = jnp.sum(cached_weight, axis=-1) + own_weight
    probs = (cached_weight / total[..., None]).astype(jnp.bfloat16)
    probs_own = (own_weight / total).astype(jnp.bfloat16)
    mixed = jnp.einsum("bkgc,bckd->bkgd", probs, stored_values, preferred_element_type=jnp.float32)
    mixed = (
        mixed
        + probs_own.astype(jnp.float32)[..., None]
        * newest_values.astype(jnp.float32)[:, :, None, :]
    )
    attended = mixed.reshape(dec, query_groups * kv_heads * HEAD_SIZE).astype(jnp.bfloat16)
    return (projected, attended)


def solution(mesh):
    in_specs = (
        P(BOTH, None),
        P(BOTH, None),
        P(),
        P(BOTH, None),
        P(BOTH, None),
        P(BOTH, None, None),
        P(BOTH, None, None),
        P(BOTH),
        P("tenant", None),
        P("tenant", None, None),
        P("tenant", None, None),
    )
    out_specs = (P(BOTH, None), P(BOTH, None))
    return jax.shard_map(body, mesh=mesh, in_specs=in_specs, out_specs=out_specs, check_vma=False)
```

```python
import math

import jax
import jax.numpy as jnp
from jax import lax
from jax.experimental import pallas as pl
from jax.experimental.pallas import tpu as pltpu
from jax.sharding import PartitionSpec as P

HEAD_SIZE = 128
adapter_scale = 2.0
VMEM = 60 * 2**20
BOTH = ("replica", "tenant")


def cost(flops, bytes_accessed):
    return pl.CostEstimate(flops=flops, bytes_accessed=bytes_accessed, transcendentals=0)


def cost(flops, bytes_accessed):
    return pl.CostEstimate(flops=flops, bytes_accessed=bytes_accessed, transcendentals=0)


def split_columns(prefill, decode, tenants, owner, down, place, steps, kk, reps, sides, flips, pad):
    rows, dec = prefill.shape[0], decode.shape[0]
    ranks = down.shape[0]
    wide = steps * kk
    slots_all = owner.shape[0]

    def spot(rep, y, m, j):
        other = (y * reps + rep) ^ m
        return ((j // 2 * sides + other // reps) * 2 + j % 2) * reps + other % reps

    if kk % 128:
        stacked = jnp.concatenate([prefill, decode], axis=0)
        hot = tenants.reshape(rows, 1) == jnp.arange(slots_all, dtype=jnp.int32)[None, :]
        slots = jnp.sum(jnp.where(hot, owner[None, :], 0), axis=1).astype(jnp.bfloat16)
        slots = jnp.broadcast_to(jnp.pad(slots, (0, wide - rows))[None, :], (pad, wide))

        def pick(a, m):
            cut = a.reshape(a.shape[0], -1, kk)
            order = spot(place[0], place[1], m, jnp.arange(steps, dtype=jnp.int32))
            return jnp.take(cut, order, axis=1).reshape(a.shape[0], wide)

        return (
            [jnp.concatenate([pick(stacked, m), slots], axis=0) for m in range(4)],
            [pick(down, m) for m in flips],
        )
    count = len(flips)
    turns = 2
    each = steps // turns

    def kernel(here, own, pre, dcd, ten, dwn, *outs):
        turn = pl.program_id(0)
        slot = jnp.zeros((1, rows), jnp.float32)
        for s in range(slots_all):
            slot = jnp.where(ten[...] == s, own[s].astype(jnp.float32), slot)
        slot = jnp.broadcast_to(slot, (pad, rows)).astype(jnp.bfloat16)
        slot = jnp.concatenate([slot] + [jnp.zeros_like(slot)] * (each * kk // rows - 1), axis=1)
        for m in range(4):
            for i in range(each):
                at = spot(here[0], here[1], m, turn * each + i)
                at = pl.ds(pl.multiple_of(at * kk, kk), kk)
                to = slice(i * kk, (i + 1) * kk)
                outs[m][0:rows, to] = pre[:, at]
                below = jnp.concatenate([dcd[:, at], slot[:, to]], axis=0)
                outs[m][rows : rows + dec + pad, to] = below
                if m in flips:
                    outs[4 + flips.index(m)][:, to] = dwn[:, at]

    out = lambda j, *_: (0, j)
    whole = lambda j, *_: (0, 0)
    outs = pl.pallas_call(
        kernel,
        grid_spec=pltpu.PrefetchScalarGridSpec(
            num_scalar_prefetch=2,
            grid=(turns,),
            in_specs=[pl.BlockSpec(a.shape, whole) for a in (prefill, decode, tenants, down)],
            out_specs=[pl.BlockSpec((rows + dec + pad, each * kk), out)] * 4
            + [pl.BlockSpec((ranks, each * kk), out)] * count,
        ),
        out_shape=[jax.ShapeDtypeStruct((rows + dec + pad, wide), jnp.bfloat16)] * 4
        + [jax.ShapeDtypeStruct((ranks, wide), jnp.bfloat16)] * count,
        compiler_params=pltpu.CompilerParams(vmem_limit_bytes=VMEM),
        cost_estimate=cost(0, 10 * 2**20),
        name="split_columns",
    )(place, owner, prefill, decode, tenants, down)
    return list(outs[:4]), list(outs[4:])


def base_products(blocks, parts, spots, rows):
    kk, out_width = parts[0].shape
    tall = blocks[0].shape[0]
    n = len(parts)
    kinds = [jnp.float32] + [jnp.bfloat16] * (len(blocks) - 1)
    if kk % 128:
        quarter = jnp.zeros((n * kk, out_width), jnp.bfloat16)
        for i in range(n):
            quarter = lax.dynamic_update_slice_in_dim(quarter, parts[i], spots[i] * kk, axis=0)
        products = [jnp.dot(b, quarter, preferred_element_type=jnp.float32) for b in blocks]
        return (
            [p[:rows].astype(kind) for p, kind in zip(products, kinds)],
            [p[rows:] for p in products],
        )
    count = len(blocks)
    cut = 256

    def kernel(spot, *refs):
        xs, weights = refs[:count], refs[count : count + n]
        outs, rest = refs[count + n : 2 * count + n], refs[2 * count + n : -2]
        left, right = refs[-2:]

        @pl.when(pl.program_id(0) == 0)
        def _():
            for m in range(count):
                left[m * tall : (m + 1) * tall] = xs[m][...]

        for i in range(n):
            right[pl.ds(pl.multiple_of(spot[i] * kk, kk), kk), :] = weights[i][...]
        total = jnp.dot(left[...], right[...], preferred_element_type=jnp.float32)
        for m in range(count):
            outs[m][...] = total[m * tall : m * tall + rows].astype(kinds[m])
            rest[m][...] = total[m * tall + rows : (m + 1) * tall]

    outs = pl.pallas_call(
        kernel,
        grid_spec=pltpu.PrefetchScalarGridSpec(
            num_scalar_prefetch=1,
            grid=(out_width // cut,),
            in_specs=[pl.BlockSpec(blocks[0].shape, lambda j, s: (0, 0))] * count
            + [pl.BlockSpec((kk, cut), lambda j, s: (0, j))] * n,
            out_specs=[pl.BlockSpec((rows, cut), lambda j, s: (0, j))] * count
            + [pl.BlockSpec((tall - rows, cut), lambda j, s: (0, j))] * count,
            scratch_shapes=[
                pltpu.VMEM((count * tall, n * kk), jnp.bfloat16),
                pltpu.VMEM((n * kk, cut), jnp.bfloat16),
            ],
        ),
        out_shape=[jax.ShapeDtypeStruct((rows, out_width), kind) for kind in kinds]
        + [jax.ShapeDtypeStruct((tall - rows, out_width), jnp.float32)] * count,
        compiler_params=pltpu.CompilerParams(vmem_limit_bytes=VMEM),
        cost_estimate=cost(2 * count * tall * n * kk * out_width, (count * tall + out_width) * 2 * n * kk),
        name="base_products",
    )(spots, *blocks, *parts)
    return list(outs[:count]), list(outs[count:])


def lowered_products(blocks, pieces, columns, rows, first, rank, after):
    wide = blocks[0].shape[1]
    ranks = pieces[0].shape[0]
    total_ranks = len(pieces) * ranks
    count = len(blocks)
    folds = 128 // rank
    n = len(pieces)
    tall = rows // folds
    if n > 16:
        sums = []
        down = jnp.concatenate(pieces, axis=0)
        for b in blocks:
            product = lax.dot_general(
                b[:rows], down, (((1,), (1,)), ((), ())), preferred_element_type=jnp.float32
            )
            slot = b[first, :rows].astype(jnp.float32)
            kept = jnp.where(slot[:, None] == columns, product, 0.0)
            kept = sum(kept[:, i : i + rank] for i in range(0, total_ranks, rank))
            sums.append(jnp.concatenate(jnp.split(kept, folds, axis=0), axis=1))
        return sums
    base_row = first // 16 * 16

    def kernel(_, *refs):
        xs, ds = refs[:count], refs[count : count + n]
        col, outs, left = refs[count + n], refs[count + n + 1 : -1], refs[-1]
        slot = []
        for m in range(count):
            left[m * rows : (m + 1) * rows] = xs[m][:rows]
            slot.append(xs[m][base_row : base_row + 16, :rows].astype(jnp.float32))
        slot = [jnp.transpose(s)[:, first - base_row : first - base_row + 1] for s in slot]
        slot = jnp.broadcast_to(jnp.concatenate(slot, axis=0), (count * rows, 128))
        kept = None
        for i in range(0, n, 2):
            down = jnp.concatenate([d[...] for d in ds[i : i + 2]], axis=0)
            term = lax.dot_general(
                left[...], down, (((1,), (1,)), ((), ())), preferred_element_type=jnp.float32
            )
            for h in range(0, 2 * ranks, 128):
                at = i * ranks + h
                part = jnp.where(slot == col[0:1, at : at + 128], term[:, h : h + 128], 0.0)
                kept = part if kept is None else kept + part
        kept = kept + pltpu.roll(kept, rank, 1)
        kept = kept + pltpu.roll(kept, 2 * rank, 1)
        lane = lax.broadcasted_iota(jnp.int32, (tall, 128), 1) // rank
        for m in range(count):
            packed = jnp.zeros((tall, 128), jnp.float32)
            for b in range(folds):
                at = m * rows + b * tall
                packed = jnp.where(lane == b, kept[at : at + tall], packed)
            outs[m][...] = packed

    whole = lambda j: (0, 0)
    return pl.pallas_call(
        kernel,
        grid=(1,),
        in_specs=[pl.BlockSpec(memory_space=pl.ANY)]
        + [pl.BlockSpec(blocks[0].shape, whole)] * count
        + [pl.BlockSpec((ranks, wide), whole)] * n
        + [pl.BlockSpec(columns.shape, whole)],
        out_specs=[pl.BlockSpec((tall, 128), whole)] * count,
        out_shape=[jax.ShapeDtypeStruct((tall, 128), jnp.float32)] * count,
        scratch_shapes=[pltpu.VMEM((count * rows, wide), jnp.bfloat16)],
        compiler_params=pltpu.CompilerParams(vmem_limit_bytes=VMEM),
        cost_estimate=cost(2 * count * rows * wide * total_ranks, (count * rows + total_ranks) * 2 * wide),
        name="lowered_products",
    )(after, *blocks, *pieces, columns)


def finish(parts, block, ups, columns, bases, rows, first, rank):
    packed_rows = parts[0].shape[0]
    folds = rows // packed_rows
    out_width = bases[0].shape[1]
    n = len(ups)
    tall = ups[0].shape[0]
    base_row = first // 16 * 16
    if n * tall > 2048:
        lowered = sum(parts[1:], parts[0]).astype(jnp.bfloat16)
        lowered = jnp.concatenate(
            [lowered[:, b * rank : (b + 1) * rank] for b in range(folds)], axis=0
        )
        slot = block[first, :rows].astype(jnp.float32)
        spread = jnp.where(
            slot[:, None] == columns, jnp.tile(lowered, (1, n * tall // rank)), jnp.bfloat16(0)
        )
        up = jnp.concatenate(ups, axis=0)
        delta = jnp.dot(spread, up, preferred_element_type=jnp.float32).astype(jnp.bfloat16)
        base = sum(b.astype(jnp.float32) for b in bases)[:rows]
        return (base + adapter_scale * delta.astype(jnp.float32)).astype(jnp.bfloat16)
    cut = 256

    def kernel(*refs):
        packs = refs[:4]
        blk, col = refs[4:6]
        bas, upr = refs[6:10], refs[10 : 10 + n]
        out, wide = refs[10 + n :]

        @pl.when(pl.program_id(0) == 0)
        def _():
            slot = jnp.transpose(blk[...].astype(jnp.float32))
            slot = slot[:, first - base_row : first - base_row + 1]
            packed = (packs[0][...] + packs[1][...]) + (packs[2][...] + packs[3][...])
            lane = lax.broadcasted_iota(jnp.int32, packed.shape, 1) // rank
            spread = []
            for b in range(folds):
                one = jnp.where(lane == b, packed, 0.0)
                one = one + pltpu.roll(one, rank, 1)
                one = one + pltpu.roll(one, 2 * rank, 1)
                spread.append(one)
            lowered = jnp.concatenate(spread, axis=0)
            for i in range(0, n * tall, 128):
                kept = jnp.where(slot == col[0:1, i : i + 128], lowered, 0.0)
                wide[:, i : i + 128] = kept.astype(jnp.bfloat16)

        up = jnp.concatenate([u[...] for u in upr], axis=0)
        delta = jnp.dot(wide[...], up, preferred_element_type=jnp.float32)
        base = bas[0][0:rows]
        for b in bas[1:]:
            base = base + b[0:rows].astype(jnp.float32)
        out[...] = (base + adapter_scale * delta.astype(jnp.bfloat16).astype(jnp.float32)).astype(
            jnp.bfloat16
        )

    one = lambda j: (0, 0)
    column = lambda j: (0, j)
    return pl.pallas_call(
        kernel,
        grid=(out_width // cut,),
        in_specs=[pl.BlockSpec(parts[0].shape, one)] * 4
        + [
            pl.BlockSpec((16, rows), lambda j: (base_row // 16, 0)),
            pl.BlockSpec(columns.shape, one),
        ]
        + [pl.BlockSpec((bases[0].shape[0], cut), column)] * 4
        + [pl.BlockSpec((tall, cut), column)] * n,
        out_specs=pl.BlockSpec((rows, cut), column),
        out_shape=jax.ShapeDtypeStruct((rows, out_width), jnp.bfloat16),
        scratch_shapes=[pltpu.VMEM((rows, n * tall), jnp.bfloat16)],
        compiler_params=pltpu.CompilerParams(vmem_limit_bytes=VMEM),
        cost_estimate=cost(2 * rows * n * tall * out_width, 5 * 2**20),
        name="finish",
    )(*parts, block, columns, *bases, *ups)


def body(
    prefill_rows,
    tenant_ids,
    owner_slot,
    decode_rows,
    queries,
    key_store_cache,
    value_store_cache,
    context_len,
    base_weight,
    adapter_down,
    adapter_up,
):
    reps, peers = lax.axis_size("replica"), lax.axis_size("tenant")
    planes = reps * peers // 8
    sides = peers // (2 * planes)
    local_slots, rank, width = adapter_down.shape
    slots_all = local_slots * peers
    rows, dec = prefill_rows.shape[0], decode_rows.shape[0]
    out_width = base_weight.shape[1]
    half_width = out_width // 2
    kk = base_weight.shape[0] // reps
    steps = 2 * planes
    quarter = steps * kk
    pad = 16 - dec % 16
    r, t = lax.axis_index("replica"), lax.axis_index("tenant")
    z, y, c = t // (2 * sides), (t // 2) % sides, t % 2
    q = y * reps + r

    order = list(range(0, planes, 2)) + list(range(1, planes, 2))[::-1]
    after = {order[i]: order[(i + 1) % planes] for i in range(planes)}
    everyone = [(a, b) for a in range(reps) for b in range(peers)]

    def flip(m):
        pairs = []
        for a, b in everyone:
            other = (((b // 2) % sides) * reps + a) ^ m
            to = (b // (2 * sides) * sides + other // reps) * 2 + b % 2
            pairs.append((a * peers + b, (other % reps) * peers + to))
        return pairs

    flips = {m: flip(m) for m in (1, 2, 3)}
    ring = [
        (a * peers + b, a * peers + after[b // (2 * sides)] * 2 * sides + b % (2 * sides))
        for a, b in everyone
    ]
    cores = [(a * peers + b, a * peers + (b ^ 1)) for a, b in everyone]

    def send(value, pairs):
        return lax.ppermute(value, BOTH, pairs)

    place = jnp.where(z % 2 == 0, z // 2, planes - 1 - z // 2)

    def plane_of(k):
        spot = (place - k + planes) % planes
        return jnp.where(spot < planes // 2, 2 * spot, 2 * (planes - 1 - spot) + 1)

    spots = jnp.arange(steps, dtype=jnp.int32)
    spots = plane_of(spots // 2) * 2 + (c ^ (spots % 2))
    ranks = local_slots * rank

    def both(value):
        return [value, send(value, cores)]

    def phase(*values):
        return lax.optimization_barrier(values)

    def paired(near, far):
        return near if far is None else jnp.concatenate([near, far], axis=0)

    bases = [lax.dynamic_slice_in_dim(base_weight, r * kk, kk, axis=0)]
    bases.append(send(bases[0], ring))
    up = adapter_up.reshape(ranks, out_width)
    ups = [paired(up, send(up, flips[reps]) if sides == 2 else None)]
    ups.append(send(ups[0], ring))
    messages, downs = split_columns(
        prefill_rows,
        decode_rows,
        tenant_ids.reshape(1, rows),
        owner_slot,
        adapter_down.reshape(ranks, width),
        jnp.stack([r, y]),
        steps,
        kk,
        reps,
        sides,
        [0, reps] if sides == 2 else [0],
        pad,
    )
    near = [send(messages[m], flips[m]) for m in (1, 2)]
    down_far = send(downs[1], flips[reps]) if sides == 2 else None
    bases, ups, down_far = phase(bases, ups, down_far)

    downs = [paired(downs[0], down_far)]
    bases.append(send(bases[-1], ring))
    downs.append(send(downs[-1], ring))
    base_parts = both(bases[0]) + both(bases[1])
    near, bases, downs, base_parts, far = phase(near, bases, downs, base_parts, messages[3])

    far = send(far, flips[3])
    while len(bases) < planes:
        bases.append(send(bases[-1], ring))
    downs.append(send(downs[-1], ring))
    for held in bases[2:-1]:
        base_parts = base_parts + both(held)
    pieces = both(downs[0]) + both(downs[1])
    near, far, bases, downs, base_parts, pieces = phase(
        near, far, bases, downs, base_parts, pieces
    )

    blocks = [messages[0], *near, far]
    base_parts = base_parts + both(bases[-1])
    partials, fresh = base_products(blocks, base_parts, spots, rows)
    while len(downs) < planes:
        downs.append(send(downs[-1], ring))
    partials, fresh, downs, pieces = phase(partials, fresh, downs, pieces)

    fresh = [fresh[0]] + [send(fresh[m], flips[m]) for m in (1, 2, 3)]
    recent_output = sum(fresh[1:], fresh[0])[:dec].astype(jnp.bfloat16)
    base = [partials[0]] + [send(partials[m], flips[m]) for m in (1, 2, 3)]
    while len(ups) < planes - 1:
        ups.append(send(ups[-1], ring))
    pieces = pieces + sum([both(d) for d in downs[2:]], [])
    ups, pieces = phase(ups, pieces)
    ups.append(send(ups[-1], ring))
    up_parts = sum([both(u) for u in ups], [])

    group = jnp.arange(slots_all, dtype=jnp.int32)
    inner = group % local_slots
    side = (group // local_slots) % sides
    core = (group // (local_slots * sides)) % 2
    step = group // (local_slots * sides * 2)
    column_slot = ((plane_of(step) * sides + (y ^ side)) * 2 + (c ^ core)) * local_slots + inner
    columns = jnp.repeat(column_slot, rank).astype(jnp.float32)[None, :]
    first = rows + dec
    packed = lowered_products(blocks, pieces, columns, rows, first, rank, partials[3])
    packed = [packed[0]] + [send(packed[m], flips[m]) for m in (1, 2, 3)]
    projected = finish(packed, messages[0], up_parts, columns, base, rows, first, rank)

    kv_heads = half_width // HEAD_SIZE
    query_groups = queries.shape[1] // half_width
    positions = key_store_cache.shape[1]
    newest_keys = recent_output[:, :half_width].reshape(dec, kv_heads, HEAD_SIZE)
    newest_values = recent_output[:, half_width:].reshape(dec, kv_heads, HEAD_SIZE)
    query_head_rows = queries.reshape(dec, kv_heads, query_groups, HEAD_SIZE)
    stored_keys = key_store_cache.reshape(dec, positions, kv_heads, HEAD_SIZE)
    stored_values = value_store_cache.reshape(dec, positions, kv_heads, HEAD_SIZE)
    scale = 1.0 / math.sqrt(HEAD_SIZE)
    scores = (
        jnp.einsum(
            "bkgd,bckd->bkgc", query_head_rows, stored_keys, preferred_element_type=jnp.float32
        )
        * scale
    )
    own_score = (
        jnp.einsum(
            "bkgd,bkd->bkg", query_head_rows, newest_keys, preferred_element_type=jnp.float32
        )
        * scale
    )
    live = jnp.arange(positions, dtype=jnp.int32)[None, :] < context_len[:, None]
    scores = jnp.where(live[:, None, None, :], scores, -jnp.inf)
    top = jnp.maximum(jnp.max(scores, axis=-1), own_score)
    cached_weight = jnp.exp(scores - top[..., None])
    own_weight = jnp.exp(own_score - top)
    total = jnp.sum(cached_weight, axis=-1) + own_weight
    probs = (cached_weight / total[..., None]).astype(jnp.bfloat16)
    probs_own = (own_weight / total).astype(jnp.bfloat16)
    mixed = jnp.einsum("bkgc,bckd->bkgd", probs, stored_values, preferred_element_type=jnp.float32)
    mixed = (
        mixed
        + probs_own.astype(jnp.float32)[..., None]
        * newest_values.astype(jnp.float32)[:, :, None, :]
    )
    attended = mixed.reshape(dec, query_groups * kv_heads * HEAD_SIZE).astype(jnp.bfloat16)
    return (projected, attended)


def solution(mesh):
    in_specs = (
        P(BOTH, None),
        P(BOTH, None),
        P(),
        P(BOTH, None),
        P(BOTH, None),
        P(BOTH, None, None),
        P(BOTH, None, None),
        P(BOTH),
        P("tenant", None),
        P("tenant", None, None),
        P("tenant", None, None),
    )
    out_specs = (P(BOTH, None), P(BOTH, None))
    return jax.shard_map(body, mesh=mesh, in_specs=in_specs, out_specs=out_specs, check_vma=False)
```

```python
import math

import jax
import jax.numpy as jnp
from jax import lax
from jax.experimental import pallas as pl
from jax.experimental.pallas import tpu as pltpu
from jax.sharding import PartitionSpec as P

HEAD_SIZE = 128
adapter_scale = 2.0
VMEM = 60 * 2**20
BOTH = ("replica", "tenant")


def cost(flops, bytes_accessed):
    return pl.CostEstimate(flops=flops, bytes_accessed=bytes_accessed, transcendentals=0)


def cost(flops, bytes_accessed):
    return pl.CostEstimate(flops=flops, bytes_accessed=bytes_accessed, transcendentals=0)


def split_columns(prefill, decode, tenants, owner, down, place, steps, kk, reps, sides, flips, pad):
    rows, dec = prefill.shape[0], decode.shape[0]
    ranks = down.shape[0]
    wide = steps * kk
    slots_all = owner.shape[0]

    def spot(rep, y, m, j):
        other = (y * reps + rep) ^ m
        return ((j // 2 * sides + other // reps) * 2 + j % 2) * reps + other % reps

    if kk % 128:
        stacked = jnp.concatenate([prefill, decode], axis=0)
        hot = tenants.reshape(rows, 1) == jnp.arange(slots_all, dtype=jnp.int32)[None, :]
        slots = jnp.sum(jnp.where(hot, owner[None, :], 0), axis=1).astype(jnp.bfloat16)
        slots = jnp.broadcast_to(jnp.pad(slots, (0, wide - rows))[None, :], (pad, wide))

        def pick(a, m):
            cut = a.reshape(a.shape[0], -1, kk)
            order = spot(place[0], place[1], m, jnp.arange(steps, dtype=jnp.int32))
            return jnp.take(cut, order, axis=1).reshape(a.shape[0], wide)

        return (
            [jnp.concatenate([pick(stacked, m), slots], axis=0) for m in range(4)],
            [pick(down, m) for m in flips],
        )
    count = len(flips)
    turns = 2
    each = steps // turns

    def kernel(here, own, pre, dcd, ten, dwn, *outs):
        turn = pl.program_id(0)
        slot = jnp.zeros((1, rows), jnp.float32)
        for s in range(slots_all):
            slot = jnp.where(ten[...] == s, own[s].astype(jnp.float32), slot)
        slot = jnp.broadcast_to(slot, (pad, rows)).astype(jnp.bfloat16)
        slot = jnp.concatenate([slot] + [jnp.zeros_like(slot)] * (each * kk // rows - 1), axis=1)
        for m in range(4):
            for i in range(each):
                at = spot(here[0], here[1], m, turn * each + i)
                at = pl.ds(pl.multiple_of(at * kk, kk), kk)
                to = slice(i * kk, (i + 1) * kk)
                outs[m][0:rows, to] = pre[:, at]
                below = jnp.concatenate([dcd[:, at], slot[:, to]], axis=0)
                outs[m][rows : rows + dec + pad, to] = below
                if m in flips:
                    outs[4 + flips.index(m)][:, to] = dwn[:, at]

    out = lambda j, *_: (0, j)
    whole = lambda j, *_: (0, 0)
    outs = pl.pallas_call(
        kernel,
        grid_spec=pltpu.PrefetchScalarGridSpec(
            num_scalar_prefetch=2,
            grid=(turns,),
            in_specs=[pl.BlockSpec(a.shape, whole) for a in (prefill, decode, tenants, down)],
            out_specs=[pl.BlockSpec((rows + dec + pad, each * kk), out)] * 4
            + [pl.BlockSpec((ranks, each * kk), out)] * count,
        ),
        out_shape=[jax.ShapeDtypeStruct((rows + dec + pad, wide), jnp.bfloat16)] * 4
        + [jax.ShapeDtypeStruct((ranks, wide), jnp.bfloat16)] * count,
        compiler_params=pltpu.CompilerParams(vmem_limit_bytes=VMEM),
        cost_estimate=cost(0, 10 * 2**20),
        name="split_columns",
    )(place, owner, prefill, decode, tenants, down)
    return list(outs[:4]), list(outs[4:])


def base_products(blocks, parts, spots):
    kk, out_width = parts[0].shape
    tall = blocks[0].shape[0]
    n = len(parts)
    kinds = [jnp.float32] + [jnp.bfloat16] * (len(blocks) - 1)
    if kk % 128:
        quarter = jnp.zeros((n * kk, out_width), jnp.bfloat16)
        for i in range(n):
            quarter = lax.dynamic_update_slice_in_dim(quarter, parts[i], spots[i] * kk, axis=0)
        products = [jnp.dot(b, quarter, preferred_element_type=jnp.float32) for b in blocks]
        return [p.astype(kind) for p, kind in zip(products, kinds)]
    count = len(blocks)
    cut = 256

    def kernel(spot, *refs):
        xs, weights = refs[:count], refs[count : count + n]
        outs = refs[count + n : 2 * count + n]
        left, right = refs[-2:]

        @pl.when(pl.program_id(0) == 0)
        def _():
            for m in range(count):
                left[m * tall : (m + 1) * tall] = xs[m][...]

        for i in range(n):
            right[pl.ds(pl.multiple_of(spot[i] * kk, kk), kk), :] = weights[i][...]
        total = jnp.dot(left[...], right[...], preferred_element_type=jnp.float32)
        for m in range(count):
            outs[m][...] = total[m * tall : (m + 1) * tall].astype(kinds[m])

    outs = pl.pallas_call(
        kernel,
        grid_spec=pltpu.PrefetchScalarGridSpec(
            num_scalar_prefetch=1,
            grid=(out_width // cut,),
            in_specs=[pl.BlockSpec(blocks[0].shape, lambda j, s: (0, 0))] * count
            + [pl.BlockSpec((kk, cut), lambda j, s: (0, j))] * n,
            out_specs=[pl.BlockSpec((tall, cut), lambda j, s: (0, j))] * count,
            scratch_shapes=[
                pltpu.VMEM((count * tall, n * kk), jnp.bfloat16),
                pltpu.VMEM((n * kk, cut), jnp.bfloat16),
            ],
        ),
        out_shape=[jax.ShapeDtypeStruct((tall, out_width), kind) for kind in kinds],
        compiler_params=pltpu.CompilerParams(vmem_limit_bytes=28 * 2**20),
        cost_estimate=cost(2 * count * tall * n * kk * out_width, (count * tall + out_width) * 2 * n * kk),
        name="base_products",
    )(spots, *blocks, *parts)
    return list(outs)


def lowered_products(blocks, pieces, columns, rows, first, rank, after):
    wide = blocks[0].shape[1]
    ranks = pieces[0].shape[0]
    total_ranks = len(pieces) * ranks
    count = len(blocks)
    folds = 128 // rank
    n = len(pieces)
    tall = rows // folds
    if n > 16:
        sums = []
        down = jnp.concatenate(pieces, axis=0)
        for b in blocks:
            product = lax.dot_general(
                b[:rows], down, (((1,), (1,)), ((), ())), preferred_element_type=jnp.float32
            )
            slot = b[first, :rows].astype(jnp.float32)
            kept = jnp.where(slot[:, None] == columns, product, 0.0)
            kept = sum(kept[:, i : i + rank] for i in range(0, total_ranks, rank))
            sums.append(jnp.concatenate(jnp.split(kept, folds, axis=0), axis=1))
        return sums
    base_row = first // 16 * 16

    def kernel(_, *refs):
        xs, ds = refs[:count], refs[count : count + n]
        col, outs, left = refs[count + n], refs[count + n + 1 : -1], refs[-1]
        slot = []
        for m in range(count):
            left[m * rows : (m + 1) * rows] = xs[m][:rows]
            slot.append(xs[m][base_row : base_row + 16, :rows].astype(jnp.float32))
        slot = [jnp.transpose(s)[:, first - base_row : first - base_row + 1] for s in slot]
        slot = jnp.broadcast_to(jnp.concatenate(slot, axis=0), (count * rows, 128))
        kept = None
        for i in range(0, n, 2):
            down = jnp.concatenate([d[...] for d in ds[i : i + 2]], axis=0)
            term = lax.dot_general(
                left[...], down, (((1,), (1,)), ((), ())), preferred_element_type=jnp.float32
            )
            for h in range(0, 2 * ranks, 128):
                at = i * ranks + h
                part = jnp.where(slot == col[0:1, at : at + 128], term[:, h : h + 128], 0.0)
                kept = part if kept is None else kept + part
        kept = kept + pltpu.roll(kept, rank, 1)
        kept = kept + pltpu.roll(kept, 2 * rank, 1)
        lane = lax.broadcasted_iota(jnp.int32, (tall, 128), 1) // rank
        for m in range(count):
            packed = jnp.zeros((tall, 128), jnp.float32)
            for b in range(folds):
                at = m * rows + b * tall
                packed = jnp.where(lane == b, kept[at : at + tall], packed)
            outs[m][...] = packed

    whole = lambda j: (0, 0)
    return pl.pallas_call(
        kernel,
        grid=(1,),
        in_specs=[pl.BlockSpec(memory_space=pl.ANY)]
        + [pl.BlockSpec(blocks[0].shape, whole)] * count
        + [pl.BlockSpec((ranks, wide), whole)] * n
        + [pl.BlockSpec(columns.shape, whole)],
        out_specs=[pl.BlockSpec((tall, 128), whole)] * count,
        out_shape=[jax.ShapeDtypeStruct((tall, 128), jnp.float32)] * count,
        scratch_shapes=[pltpu.VMEM((count * rows, wide), jnp.bfloat16)],
        compiler_params=pltpu.CompilerParams(vmem_limit_bytes=32 * 2**20),
        cost_estimate=cost(2 * count * rows * wide * total_ranks, (count * rows + total_ranks) * 2 * wide),
        name="lowered_products",
    )(after, *blocks, *pieces, columns)


def finish(parts, block, ups, columns, bases, rows, first, rank):
    packed_rows = parts[0].shape[0]
    folds = rows // packed_rows
    out_width = bases[0].shape[1]
    n = len(ups)
    tall = ups[0].shape[0]
    base_row = first // 16 * 16
    if n * tall > 2048:
        lowered = sum(parts[1:], parts[0]).astype(jnp.bfloat16)
        lowered = jnp.concatenate(
            [lowered[:, b * rank : (b + 1) * rank] for b in range(folds)], axis=0
        )
        slot = block[first, :rows].astype(jnp.float32)
        spread = jnp.where(
            slot[:, None] == columns, jnp.tile(lowered, (1, n * tall // rank)), jnp.bfloat16(0)
        )
        up = jnp.concatenate(ups, axis=0)
        delta = jnp.dot(spread, up, preferred_element_type=jnp.float32).astype(jnp.bfloat16)
        base = sum(b.astype(jnp.float32) for b in bases)[:rows]
        return (base + adapter_scale * delta.astype(jnp.float32)).astype(jnp.bfloat16)
    cut = 256

    def kernel(*refs):
        packs = refs[:4]
        blk, col = refs[4:6]
        bas, upr = refs[6:10], refs[10 : 10 + n]
        out, wide = refs[10 + n :]

        @pl.when(pl.program_id(0) == 0)
        def _():
            slot = jnp.transpose(blk[...].astype(jnp.float32))
            slot = slot[:, first - base_row : first - base_row + 1]
            packed = (packs[0][...] + packs[1][...]) + (packs[2][...] + packs[3][...])
            lane = lax.broadcasted_iota(jnp.int32, packed.shape, 1) // rank
            spread = []
            for b in range(folds):
                one = jnp.where(lane == b, packed, 0.0)
                one = one + pltpu.roll(one, rank, 1)
                one = one + pltpu.roll(one, 2 * rank, 1)
                spread.append(one)
            lowered = jnp.concatenate(spread, axis=0)
            for i in range(0, n * tall, 128):
                kept = jnp.where(slot == col[0:1, i : i + 128], lowered, 0.0)
                wide[:, i : i + 128] = kept.astype(jnp.bfloat16)

        up = jnp.concatenate([u[...] for u in upr], axis=0)
        delta = jnp.dot(wide[...], up, preferred_element_type=jnp.float32)
        base = bas[0][0:rows]
        for b in bas[1:]:
            base = base + b[0:rows].astype(jnp.float32)
        out[...] = (base + adapter_scale * delta.astype(jnp.bfloat16).astype(jnp.float32)).astype(
            jnp.bfloat16
        )

    one = lambda j: (0, 0)
    column = lambda j: (0, j)
    return pl.pallas_call(
        kernel,
        grid=(out_width // cut,),
        in_specs=[pl.BlockSpec(parts[0].shape, one)] * 4
        + [
            pl.BlockSpec((16, rows), lambda j: (base_row // 16, 0)),
            pl.BlockSpec(columns.shape, one),
        ]
        + [pl.BlockSpec((bases[0].shape[0], cut), column)] * 4
        + [pl.BlockSpec((tall, cut), column)] * n,
        out_specs=pl.BlockSpec((rows, cut), column),
        out_shape=jax.ShapeDtypeStruct((rows, out_width), jnp.bfloat16),
        scratch_shapes=[pltpu.VMEM((rows, n * tall), jnp.bfloat16)],
        compiler_params=pltpu.CompilerParams(vmem_limit_bytes=VMEM),
        cost_estimate=cost(2 * rows * n * tall * out_width, 5 * 2**20),
        name="finish",
    )(*parts, block, columns, *bases, *ups)


def body(
    prefill_rows,
    tenant_ids,
    owner_slot,
    decode_rows,
    queries,
    key_store_cache,
    value_store_cache,
    context_len,
    base_weight,
    adapter_down,
    adapter_up,
):
    reps, peers = lax.axis_size("replica"), lax.axis_size("tenant")
    planes = reps * peers // 8
    sides = peers // (2 * planes)
    local_slots, rank, width = adapter_down.shape
    slots_all = local_slots * peers
    rows, dec = prefill_rows.shape[0], decode_rows.shape[0]
    out_width = base_weight.shape[1]
    half_width = out_width // 2
    kk = base_weight.shape[0] // reps
    steps = 2 * planes
    quarter = steps * kk
    pad = 16 - dec % 16
    r, t = lax.axis_index("replica"), lax.axis_index("tenant")
    z, y, c = t // (2 * sides), (t // 2) % sides, t % 2
    q = y * reps + r

    order = list(range(0, planes, 2)) + list(range(1, planes, 2))[::-1]
    after = {order[i]: order[(i + 1) % planes] for i in range(planes)}
    everyone = [(a, b) for a in range(reps) for b in range(peers)]

    def flip(m):
        pairs = []
        for a, b in everyone:
            other = (((b // 2) % sides) * reps + a) ^ m
            to = (b // (2 * sides) * sides + other // reps) * 2 + b % 2
            pairs.append((a * peers + b, (other % reps) * peers + to))
        return pairs

    flips = {m: flip(m) for m in (1, 2, 3)}
    ring = [
        (a * peers + b, a * peers + after[b // (2 * sides)] * 2 * sides + b % (2 * sides))
        for a, b in everyone
    ]
    cores = [(a * peers + b, a * peers + (b ^ 1)) for a, b in everyone]

    def send(value, pairs):
        return lax.ppermute(value, BOTH, pairs)

    place = jnp.where(z % 2 == 0, z // 2, planes - 1 - z // 2)

    def plane_of(k):
        spot = (place - k + planes) % planes
        return jnp.where(spot < planes // 2, 2 * spot, 2 * (planes - 1 - spot) + 1)

    spots = jnp.arange(steps, dtype=jnp.int32)
    spots = plane_of(spots // 2) * 2 + (c ^ (spots % 2))
    ranks = local_slots * rank

    def both(value):
        return [value, send(value, cores)]

    def phase(*values):
        return lax.optimization_barrier(values)

    def paired(near, far):
        return near if far is None else jnp.concatenate([near, far], axis=0)

    bases = [lax.dynamic_slice_in_dim(base_weight, r * kk, kk, axis=0)]
    bases.append(send(bases[0], ring))
    up = adapter_up.reshape(ranks, out_width)
    up_far = send(up, flips[reps]) if sides == 2 else None
    messages, downs = split_columns(
        prefill_rows,
        decode_rows,
        tenant_ids.reshape(1, rows),
        owner_slot,
        adapter_down.reshape(ranks, width),
        jnp.stack([r, y]),
        steps,
        kk,
        reps,
        sides,
        [0, reps] if sides == 2 else [0],
        pad,
    )
    near = [send(messages[m], flips[m]) for m in (1, 2)]
    down_far = send(downs[1], flips[reps]) if sides == 2 else None
    bases, up_far = phase(bases, up_far)

    kv_heads = half_width // HEAD_SIZE
    query_groups = queries.shape[1] // half_width
    positions = key_store_cache.shape[1]
    query_head_rows = queries.reshape(dec, kv_heads, query_groups, HEAD_SIZE)
    stored_keys = key_store_cache.reshape(dec, positions, kv_heads, HEAD_SIZE)
    stored_values = value_store_cache.reshape(dec, positions, kv_heads, HEAD_SIZE)
    scale = 1.0 / math.sqrt(HEAD_SIZE)
    scores = (
        jnp.einsum(
            "bkgd,bckd->bkgc", query_head_rows, stored_keys, preferred_element_type=jnp.float32
        )
        * scale
    )
    live = jnp.arange(positions, dtype=jnp.int32)[None, :] < context_len[:, None]
    scores = jnp.where(live[:, None, None, :], scores, -jnp.inf)
    cached_top = jnp.max(scores, axis=-1)
    cached_weight = jnp.exp(scores - cached_top[..., None])
    cached_total = jnp.sum(cached_weight, axis=-1)
    cached_mix = jnp.einsum(
        "bkgc,bckd->bkgd",
        cached_weight.astype(jnp.bfloat16),
        stored_values,
        preferred_element_type=jnp.float32,
    )

    group = jnp.arange(slots_all, dtype=jnp.int32)
    inner = group % local_slots
    side = (group // local_slots) % sides
    core = (group // (local_slots * sides)) % 2
    step = group // (local_slots * sides * 2)
    column_slot = ((plane_of(step) * sides + (y ^ side)) * 2 + (c ^ core)) * local_slots + inner
    columns = jnp.repeat(column_slot, rank).astype(jnp.float32)[None, :]

    downs = [paired(downs[0], down_far)]
    bases.append(send(bases[-1], ring))
    downs.append(send(downs[-1], ring))
    ups = [paired(up, up_far)]
    base_parts = both(bases[0]) + both(bases[1])
    near, bases, downs, ups, base_parts, far, cached_top, cached_total, cached_mix, columns, spots = phase(
        near,
        bases,
        downs,
        ups,
        base_parts,
        messages[3],
        cached_top,
        cached_total,
        cached_mix,
        columns,
        spots,
    )

    far = send(far, flips[3])
    while len(bases) < planes:
        bases.append(send(bases[-1], ring))
    downs.append(send(downs[-1], ring))
    ups.append(send(ups[-1], ring))
    for held in bases[2:-1]:
        base_parts = base_parts + both(held)
    pieces = both(downs[0]) + both(downs[1])
    up_parts = both(ups[0])
    near, far, bases, downs, ups, base_parts, pieces, up_parts = phase(
        near, far, bases, downs, ups, base_parts, pieces, up_parts
    )

    blocks = [messages[0], *near, far]
    base_parts = base_parts + both(bases[-1])
    partials = base_products(blocks, base_parts, spots)
    while len(downs) < planes:
        downs.append(send(downs[-1], ring))
    pieces = pieces + sum([both(d) for d in downs[2:-1]], [])
    partials, downs, pieces, ups = phase(partials, downs, pieces, ups)

    base = [partials[0]] + [send(partials[m], flips[m]) for m in (1, 2)]
    while len(ups) < planes - 1:
        ups.append(send(ups[-1], ring))
    pieces = pieces + both(downs[-1])
    up_parts = up_parts + both(ups[1])
    base, ups, up_parts, pieces, last = phase(base, ups, up_parts, pieces, partials[3])

    base.append(send(last, flips[3]))
    ups.append(send(ups[-1], ring))
    up_parts = up_parts + sum([both(u) for u in ups[2:-1]], [])

    first = rows + dec
    packed = lowered_products(blocks, pieces, columns, rows, first, rank, last)
    packed, ups, up_parts = phase(packed, ups, up_parts)
    packed = [packed[0]] + [send(packed[m], flips[m]) for m in (1, 2, 3)]
    up_parts = up_parts + both(ups[-1])

    recent_output = sum(b[rows : rows + dec].astype(jnp.float32) for b in base).astype(jnp.bfloat16)
    newest_keys = recent_output[:, :half_width].reshape(dec, kv_heads, HEAD_SIZE)
    newest_values = recent_output[:, half_width:].reshape(dec, kv_heads, HEAD_SIZE)
    own_score = (
        jnp.sum(
            query_head_rows.astype(jnp.float32) * newest_keys.astype(jnp.float32)[:, :, None, :],
            axis=-1,
        )
        * scale
    )
    top = jnp.maximum(cached_top, own_score)
    kept = jnp.exp(cached_top - top)
    own_weight = jnp.exp(own_score - top)
    total = kept * cached_total + own_weight
    mixed = (
        kept[..., None] * cached_mix
        + own_weight[..., None] * newest_values.astype(jnp.float32)[:, :, None, :]
    ) / total[..., None]
    attended = mixed.reshape(dec, query_groups * half_width).astype(jnp.bfloat16)

    projected = finish(packed, messages[0], up_parts, columns, base, rows, first, rank)
    return (projected, attended)


def solution(mesh):
    in_specs = (
        P(BOTH, None),
        P(BOTH, None),
        P(),
        P(BOTH, None),
        P(BOTH, None),
        P(BOTH, None, None),
        P(BOTH, None, None),
        P(BOTH),
        P("tenant", None),
        P("tenant", None, None),
        P("tenant", None, None),
    )
    out_specs = (P(BOTH, None), P(BOTH, None))
    return jax.shard_map(body, mesh=mesh, in_specs=in_specs, out_specs=out_specs, check_vma=False)
```

```python
import math

import jax
import jax.numpy as jnp
from jax import lax
from jax.experimental import pallas as pl
from jax.experimental.pallas import tpu as pltpu
from jax.sharding import PartitionSpec as P

HEAD_SIZE = 128
adapter_scale = 2.0
VMEM = 60 * 2**20
BOTH = ("replica", "tenant")


def cost(flops, bytes_accessed):
    return pl.CostEstimate(flops=flops, bytes_accessed=bytes_accessed, transcendentals=0)


def cost(flops, bytes_accessed):
    return pl.CostEstimate(flops=flops, bytes_accessed=bytes_accessed, transcendentals=0)


def column_spot(rep, y, m, j, reps, sides):
    other = (y * reps + rep) ^ m
    return ((j // 2 * sides + other // reps) * 2 + j % 2) * reps + other % reps


def split_down(down, place, steps, kk, reps, sides, flips):
    ranks = down.shape[0]
    wide = steps * kk
    if kk % 128:

        def pick(m):
            cut = down.reshape(ranks, -1, kk)
            order = jnp.arange(steps, dtype=jnp.int32)
            order = column_spot(place[0], place[1], m, order, reps, sides)
            return jnp.take(cut, order, axis=1).reshape(ranks, wide)

        return [pick(m) for m in flips]

    def kernel(here, dwn, *outs):
        for i, m in enumerate(flips):
            for j in range(steps):
                at = column_spot(here[0], here[1], m, j, reps, sides)
                outs[i][:, j * kk : (j + 1) * kk] = dwn[:, pl.ds(pl.multiple_of(at * kk, kk), kk)]

    whole = lambda j, *_: (0, 0)
    return pl.pallas_call(
        kernel,
        grid_spec=pltpu.PrefetchScalarGridSpec(
            num_scalar_prefetch=1,
            grid=(1,),
            in_specs=[pl.BlockSpec(down.shape, whole)],
            out_specs=[pl.BlockSpec((ranks, wide), whole)] * len(flips),
        ),
        out_shape=[jax.ShapeDtypeStruct((ranks, wide), jnp.bfloat16)] * len(flips),
        compiler_params=pltpu.CompilerParams(vmem_limit_bytes=VMEM),
        cost_estimate=cost(0, 2 * 2**20),
        name="split_down",
    )(place, down)


def split_columns(prefill, decode, tenants, owner, place, steps, kk, reps, sides, pad):
    rows, dec = prefill.shape[0], decode.shape[0]
    wide = steps * kk
    slots_all = owner.shape[0]
    if kk % 128:
        stacked = jnp.concatenate([prefill, decode], axis=0)
        hot = tenants.reshape(rows, 1) == jnp.arange(slots_all, dtype=jnp.int32)[None, :]
        slots = jnp.sum(jnp.where(hot, owner[None, :], 0), axis=1).astype(jnp.bfloat16)
        slots = jnp.broadcast_to(jnp.pad(slots, (0, wide - rows))[None, :], (pad, wide))

        def pick(m):
            cut = stacked.reshape(stacked.shape[0], -1, kk)
            order = jnp.arange(steps, dtype=jnp.int32)
            order = column_spot(place[0], place[1], m, order, reps, sides)
            return jnp.take(cut, order, axis=1).reshape(stacked.shape[0], wide)

        return [jnp.concatenate([pick(m), slots], axis=0) for m in range(4)]
    turns = 2
    each = steps // turns

    def kernel(here, own, pre, dcd, ten, *outs):
        turn = pl.program_id(0)
        slot = jnp.zeros((1, rows), jnp.float32)
        for s in range(slots_all):
            slot = jnp.where(ten[...] == s, own[s].astype(jnp.float32), slot)
        slot = jnp.broadcast_to(slot, (pad, rows)).astype(jnp.bfloat16)
        slot = jnp.concatenate([slot] + [jnp.zeros_like(slot)] * (each * kk // rows - 1), axis=1)
        for m in range(4):
            for i in range(each):
                at = column_spot(here[0], here[1], m, turn * each + i, reps, sides)
                at = pl.ds(pl.multiple_of(at * kk, kk), kk)
                to = slice(i * kk, (i + 1) * kk)
                outs[m][0:rows, to] = pre[:, at]
                below = jnp.concatenate([dcd[:, at], slot[:, to]], axis=0)
                outs[m][rows : rows + dec + pad, to] = below

    out = lambda j, *_: (0, j)
    whole = lambda j, *_: (0, 0)
    return pl.pallas_call(
        kernel,
        grid_spec=pltpu.PrefetchScalarGridSpec(
            num_scalar_prefetch=2,
            grid=(turns,),
            in_specs=[pl.BlockSpec(a.shape, whole) for a in (prefill, decode, tenants)],
            out_specs=[pl.BlockSpec((rows + dec + pad, each * kk), out)] * 4,
        ),
        out_shape=[jax.ShapeDtypeStruct((rows + dec + pad, wide), jnp.bfloat16)] * 4,
        compiler_params=pltpu.CompilerParams(vmem_limit_bytes=VMEM),
        cost_estimate=cost(0, 9 * 2**20),
        name="split_columns",
    )(place, owner, prefill, decode, tenants)


def base_products(blocks, parts, spots, kinds):
    kk, out_width = parts[0].shape
    tall = blocks[0].shape[0]
    n = len(parts)
    if kk % 128:
        quarter = jnp.zeros((n * kk, out_width), jnp.bfloat16)
        for i in range(n):
            quarter = lax.dynamic_update_slice_in_dim(quarter, parts[i], spots[i] * kk, axis=0)
        products = [jnp.dot(b, quarter, preferred_element_type=jnp.float32) for b in blocks]
        return [p.astype(kind) for p, kind in zip(products, kinds)]
    count = len(blocks)
    cut = 256

    def kernel(spot, *refs):
        xs, weights = refs[:count], refs[count : count + n]
        outs = refs[count + n : 2 * count + n]
        left, right = refs[-2:]

        @pl.when(pl.program_id(0) == 0)
        def _():
            for m in range(count):
                left[m * tall : (m + 1) * tall] = xs[m][...]

        for i in range(n):
            right[pl.ds(pl.multiple_of(spot[i] * kk, kk), kk), :] = weights[i][...]
        total = jnp.dot(left[...], right[...], preferred_element_type=jnp.float32)
        for m in range(count):
            outs[m][...] = total[m * tall : (m + 1) * tall].astype(kinds[m])

    outs = pl.pallas_call(
        kernel,
        grid_spec=pltpu.PrefetchScalarGridSpec(
            num_scalar_prefetch=1,
            grid=(out_width // cut,),
            in_specs=[pl.BlockSpec(blocks[0].shape, lambda j, s: (0, 0))] * count
            + [pl.BlockSpec((kk, cut), lambda j, s: (0, j))] * n,
            out_specs=[pl.BlockSpec((tall, cut), lambda j, s: (0, j))] * count,
            scratch_shapes=[
                pltpu.VMEM((count * tall, n * kk), jnp.bfloat16),
                pltpu.VMEM((n * kk, cut), jnp.bfloat16),
            ],
        ),
        out_shape=[jax.ShapeDtypeStruct((tall, out_width), kind) for kind in kinds],
        compiler_params=pltpu.CompilerParams(vmem_limit_bytes=28 * 2**20),
        cost_estimate=cost(2 * count * tall * n * kk * out_width, (count * tall + out_width) * 2 * n * kk),
        name="base_products",
    )(spots, *blocks, *parts)
    return list(outs)


def lowered_products(blocks, pieces, columns, rows, first, rank, after):
    wide = blocks[0].shape[1]
    ranks = pieces[0].shape[0]
    total_ranks = len(pieces) * ranks
    count = len(blocks)
    folds = 128 // rank
    n = len(pieces)
    tall = rows // folds
    if n > 16:
        sums = []
        down = jnp.concatenate(pieces, axis=0)
        for b in blocks:
            product = lax.dot_general(
                b[:rows], down, (((1,), (1,)), ((), ())), preferred_element_type=jnp.float32
            )
            slot = b[first, :rows].astype(jnp.float32)
            kept = jnp.where(slot[:, None] == columns, product, 0.0)
            kept = sum(kept[:, i : i + rank] for i in range(0, total_ranks, rank))
            sums.append(jnp.concatenate(jnp.split(kept, folds, axis=0), axis=1))
        return sums
    base_row = first // 16 * 16

    def kernel(_, *refs):
        xs, ds = refs[:count], refs[count : count + n]
        col, outs, left = refs[count + n], refs[count + n + 1 : -1], refs[-1]
        slot = []
        for m in range(count):
            left[m * rows : (m + 1) * rows] = xs[m][:rows]
            slot.append(xs[m][base_row : base_row + 16, :rows].astype(jnp.float32))
        slot = [jnp.transpose(s)[:, first - base_row : first - base_row + 1] for s in slot]
        slot = jnp.broadcast_to(jnp.concatenate(slot, axis=0), (count * rows, 128))
        kept = None
        for i in range(0, n, 2):
            down = jnp.concatenate([d[...] for d in ds[i : i + 2]], axis=0)
            term = lax.dot_general(
                left[...], down, (((1,), (1,)), ((), ())), preferred_element_type=jnp.float32
            )
            for h in range(0, 2 * ranks, 128):
                at = i * ranks + h
                part = jnp.where(slot == col[0:1, at : at + 128], term[:, h : h + 128], 0.0)
                kept = part if kept is None else kept + part
        kept = kept + pltpu.roll(kept, rank, 1)
        kept = kept + pltpu.roll(kept, 2 * rank, 1)
        lane = lax.broadcasted_iota(jnp.int32, (tall, 128), 1) // rank
        for m in range(count):
            packed = jnp.zeros((tall, 128), jnp.float32)
            for b in range(folds):
                at = m * rows + b * tall
                packed = jnp.where(lane == b, kept[at : at + tall], packed)
            outs[m][...] = packed

    whole = lambda j: (0, 0)
    return pl.pallas_call(
        kernel,
        grid=(1,),
        in_specs=[pl.BlockSpec(memory_space=pl.ANY)]
        + [pl.BlockSpec(blocks[0].shape, whole)] * count
        + [pl.BlockSpec((ranks, wide), whole)] * n
        + [pl.BlockSpec(columns.shape, whole)],
        out_specs=[pl.BlockSpec((tall, 128), whole)] * count,
        out_shape=[jax.ShapeDtypeStruct((tall, 128), jnp.float32)] * count,
        scratch_shapes=[pltpu.VMEM((count * rows, wide), jnp.bfloat16)],
        compiler_params=pltpu.CompilerParams(vmem_limit_bytes=32 * 2**20),
        cost_estimate=cost(2 * count * rows * wide * total_ranks, (count * rows + total_ranks) * 2 * wide),
        name="lowered_products",
    )(after, *blocks, *pieces, columns)


def own_attention(fresh, queries, tops, totals, mix):
    dec, out_width = fresh.shape
    heads = queries.shape[0] // dec
    kv_heads = out_width // 2 // HEAD_SIZE
    fresh = fresh.astype(jnp.bfloat16).astype(jnp.float32)
    parts = [fresh[:, i * HEAD_SIZE : (i + 1) * HEAD_SIZE] for i in range(2 * kv_heads)]
    group = heads // kv_heads
    keys = jnp.concatenate([parts[h // group] for h in range(heads)], axis=0)
    values = jnp.concatenate([parts[kv_heads + h // group] for h in range(heads)], axis=0)
    own = jnp.sum(queries.astype(jnp.float32) * keys, axis=1, keepdims=True)
    own = jnp.broadcast_to(own * (1.0 / math.sqrt(HEAD_SIZE)), mix.shape)
    tops, totals = jnp.broadcast_to(tops, mix.shape), jnp.broadcast_to(totals, mix.shape)
    top = jnp.maximum(tops, own)
    kept, weight = jnp.exp(tops - top), jnp.exp(own - top)
    mixed = (kept * mix + weight * values) / (kept * totals + weight)
    mixed = mixed.astype(jnp.bfloat16)
    return [mixed[h * dec : (h + 1) * dec] for h in range(heads)]


def finish(parts, block, ups, columns, bases, rows, first, rank, cached, dec):
    heads = cached[0].shape[0] // dec
    shape = (dec, heads * HEAD_SIZE)
    packed_rows = parts[0].shape[0]
    folds = rows // packed_rows
    out_width = bases[0].shape[1]
    n = len(ups)
    tall = ups[0].shape[0]
    base_row = first // 16 * 16
    if n * tall > 2048:
        lowered = sum(parts[1:], parts[0]).astype(jnp.bfloat16)
        lowered = jnp.concatenate(
            [lowered[:, b * rank : (b + 1) * rank] for b in range(folds)], axis=0
        )
        slot = block[first, :rows].astype(jnp.float32)
        spread = jnp.where(
            slot[:, None] == columns, jnp.tile(lowered, (1, n * tall // rank)), jnp.bfloat16(0)
        )
        up = jnp.concatenate(ups, axis=0)
        delta = jnp.dot(spread, up, preferred_element_type=jnp.float32).astype(jnp.bfloat16)
        base = sum(b.astype(jnp.float32) for b in bases)
        attended = own_attention(base[rows : rows + dec], *cached)
        base = base[:rows]
        projected = (base + adapter_scale * delta.astype(jnp.float32)).astype(jnp.bfloat16)
        return projected, jnp.concatenate(attended, axis=1)
    cut = 256
    below = bases[0].shape[0] - rows

    def kernel(*refs):
        packs = refs[:4]
        blk, col = refs[4:6]
        bas, upr = refs[6:10], refs[10 : 10 + n]
        own, old = refs[10 + n : 14 + n], refs[14 + n : 18 + n]
        out, out_attended, wide = refs[18 + n :]

        @pl.when(pl.program_id(0) == 0)
        def _():
            slot = jnp.transpose(blk[...].astype(jnp.float32))
            slot = slot[:, first - base_row : first - base_row + 1]
            packed = (packs[0][...] + packs[1][...]) + (packs[2][...] + packs[3][...])
            lane = lax.broadcasted_iota(jnp.int32, packed.shape, 1) // rank
            spread = []
            for b in range(folds):
                one = jnp.where(lane == b, packed, 0.0)
                one = one + pltpu.roll(one, rank, 1)
                one = one + pltpu.roll(one, 2 * rank, 1)
                spread.append(one)
            lowered = jnp.concatenate(spread, axis=0)
            for i in range(0, n * tall, 128):
                kept = jnp.where(slot == col[0:1, i : i + 128], lowered, 0.0)
                wide[:, i : i + 128] = kept.astype(jnp.bfloat16)
            fresh = own[0][...]
            for b in own[1:]:
                fresh = fresh + b[...].astype(jnp.float32)
            parts_own = own_attention(fresh[:dec], *[c[...] for c in old])
            for h in range(heads):
                out_attended[:, h * HEAD_SIZE : (h + 1) * HEAD_SIZE] = parts_own[h]

        up = jnp.concatenate([u[...] for u in upr], axis=0)
        delta = jnp.dot(wide[...], up, preferred_element_type=jnp.float32)
        base = bas[0][0:rows]
        for b in bas[1:]:
            base = base + b[0:rows].astype(jnp.float32)
        out[...] = (base + adapter_scale * delta.astype(jnp.bfloat16).astype(jnp.float32)).astype(
            jnp.bfloat16
        )

    one = lambda j: (0, 0)
    column = lambda j: (0, j)
    return pl.pallas_call(
        kernel,
        grid=(out_width // cut,),
        in_specs=[pl.BlockSpec(parts[0].shape, one)] * 4
        + [
            pl.BlockSpec((16, rows), lambda j: (base_row // 16, 0)),
            pl.BlockSpec(columns.shape, one),
        ]
        + [pl.BlockSpec((bases[0].shape[0], cut), column)] * 4
        + [pl.BlockSpec((tall, cut), column)] * n
        + [pl.BlockSpec((below, out_width), lambda j: (rows // below, 0))] * 4
        + [pl.BlockSpec(a.shape, one) for a in cached],
        out_specs=[pl.BlockSpec((rows, cut), column), pl.BlockSpec(shape, one)],
        out_shape=[
            jax.ShapeDtypeStruct((rows, out_width), jnp.bfloat16),
            jax.ShapeDtypeStruct(shape, jnp.bfloat16),
        ],
        scratch_shapes=[pltpu.VMEM((rows, n * tall), jnp.bfloat16)],
        compiler_params=pltpu.CompilerParams(vmem_limit_bytes=VMEM),
        cost_estimate=cost(2 * rows * n * tall * out_width, 5 * 2**20),
        name="finish",
    )(*parts, block, columns, *bases, *ups, *bases, *cached)


def body(
    prefill_rows,
    tenant_ids,
    owner_slot,
    decode_rows,
    queries,
    key_store_cache,
    value_store_cache,
    context_len,
    base_weight,
    adapter_down,
    adapter_up,
):
    reps, peers = lax.axis_size("replica"), lax.axis_size("tenant")
    planes = reps * peers // 8
    sides = peers // (2 * planes)
    local_slots, rank, width = adapter_down.shape
    slots_all = local_slots * peers
    rows, dec = prefill_rows.shape[0], decode_rows.shape[0]
    out_width = base_weight.shape[1]
    half_width = out_width // 2
    kk = base_weight.shape[0] // reps
    steps = 2 * planes
    quarter = steps * kk
    pad = 16 - dec % 16
    r, t = lax.axis_index("replica"), lax.axis_index("tenant")
    z, y, c = t // (2 * sides), (t // 2) % sides, t % 2
    q = y * reps + r

    order = list(range(0, planes, 2)) + list(range(1, planes, 2))[::-1]
    after = {order[i]: order[(i + 1) % planes] for i in range(planes)}
    everyone = [(a, b) for a in range(reps) for b in range(peers)]

    def flip(m):
        pairs = []
        for a, b in everyone:
            other = (((b // 2) % sides) * reps + a) ^ m
            to = (b // (2 * sides) * sides + other // reps) * 2 + b % 2
            pairs.append((a * peers + b, (other % reps) * peers + to))
        return pairs

    flips = {m: flip(m) for m in (1, 2, 3)}
    ring = [
        (a * peers + b, a * peers + after[b // (2 * sides)] * 2 * sides + b % (2 * sides))
        for a, b in everyone
    ]
    cores = [(a * peers + b, a * peers + (b ^ 1)) for a, b in everyone]

    def send(value, pairs):
        return lax.ppermute(value, BOTH, pairs)

    place = jnp.where(z % 2 == 0, z // 2, planes - 1 - z // 2)

    def plane_of(k):
        spot = (place - k + planes) % planes
        return jnp.where(spot < planes // 2, 2 * spot, 2 * (planes - 1 - spot) + 1)

    spots = jnp.arange(steps, dtype=jnp.int32)
    spots = plane_of(spots // 2) * 2 + (c ^ (spots % 2))
    ranks = local_slots * rank

    def both(value):
        return [value, send(value, cores)]

    def phase(*values):
        return lax.optimization_barrier(values)

    def paired(near, far):
        return near if far is None else jnp.concatenate([near, far], axis=0)

    bases = [lax.dynamic_slice_in_dim(base_weight, r * kk, kk, axis=0)]
    up = adapter_up.reshape(ranks, out_width)
    here, bases, up = phase(jnp.stack([r, y]), bases, up)
    bases.append(send(bases[0], ring))
    up_far = send(up, flips[reps]) if sides == 2 else None
    y_flips = [0, reps] if sides == 2 else [0]
    downs = split_down(adapter_down.reshape(ranks, width), here, steps, kk, reps, sides, y_flips)
    here, downs = phase(here, downs)
    down_far = send(downs[1], flips[reps]) if sides == 2 else None
    messages = split_columns(
        prefill_rows,
        decode_rows,
        tenant_ids.reshape(1, rows),
        owner_slot,
        here,
        steps,
        kk,
        reps,
        sides,
        pad,
    )
    downs = [paired(downs[0], down_far)]
    ups = [paired(up, up_far)]
    base_parts = both(bases[0])
    bases, downs, ups, messages, base_parts = phase(bases, downs, ups, messages, base_parts)
    near = [send(messages[m], flips[m]) for m in (1, 2)]
    message = messages[0]

    bases.append(send(bases[-1], ring))
    bases, queries = phase(bases, queries)
    while len(bases) < planes:
        bases.append(send(bases[-1], ring))
    for held in bases[1:2]:
        base_parts = base_parts + both(held)

    kv_heads = half_width // HEAD_SIZE
    query_groups = queries.shape[1] // half_width
    positions = key_store_cache.shape[1]
    query_head_rows = queries.reshape(dec, kv_heads, query_groups, HEAD_SIZE)
    stored_keys = key_store_cache.reshape(dec, positions, kv_heads, HEAD_SIZE)
    stored_values = value_store_cache.reshape(dec, positions, kv_heads, HEAD_SIZE)
    scale = 1.0 / math.sqrt(HEAD_SIZE)
    scores = (
        jnp.einsum(
            "bkgd,bckd->bkgc", query_head_rows, stored_keys, preferred_element_type=jnp.float32
        )
        * scale
    )
    live = jnp.arange(positions, dtype=jnp.int32)[None, :] < context_len[:, None]
    scores = jnp.where(live[:, None, None, :], scores, -jnp.inf)
    cached_top = jnp.max(scores, axis=-1)
    cached_weight = jnp.exp(scores - cached_top[..., None])
    cached_total = jnp.sum(cached_weight, axis=-1)
    cached_mix = jnp.einsum(
        "bkgc,bckd->bkgd",
        cached_weight.astype(jnp.bfloat16),
        stored_values,
        preferred_element_type=jnp.float32,
    )
    tall = kv_heads * query_groups * dec

    def by_head(value):
        value = value if value.ndim == 4 else value[..., None]
        return value.transpose(1, 2, 0, 3).reshape(tall, value.shape[3])

    cached = [by_head(v) for v in (query_head_rows, cached_top, cached_total, cached_mix)]

    group = jnp.arange(slots_all, dtype=jnp.int32)
    inner = group % local_slots
    side = (group // local_slots) % sides
    core = (group // (local_slots * sides)) % 2
    step = group // (local_slots * sides * 2)
    column_slot = ((plane_of(step) * sides + (y ^ side)) * 2 + (c ^ core)) * local_slots + inner
    columns = jnp.repeat(column_slot, rank).astype(jnp.float32)[None, :]
    core = group // (local_slots * sides * planes)
    step = (group // (local_slots * sides)) % planes
    column_slot = ((plane_of(step) * sides + (y ^ side)) * 2 + (c ^ core)) * local_slots + inner
    up_columns = jnp.repeat(column_slot, rank).astype(jnp.float32)[None, :]

    pieces = both(downs[0])
    near, bases, ups, far, base_parts, pieces, cached, columns, up_columns, spots = phase(
        near, bases, ups, messages[3], base_parts, pieces, cached, columns, up_columns, spots
    )

    far = send(far, flips[3])
    while len(downs) < max(2, planes - 1):
        downs.append(send(downs[-1], ring))
    for held in bases[2:]:
        base_parts = base_parts + both(held)
    partials = base_products(near, base_parts, spots, [jnp.bfloat16] * 2)
    up_cores = [send(ups[0], cores)]
    pieces = pieces + both(downs[1])
    far, downs, ups, partials, base_parts, up_cores, pieces = phase(
        far, downs, ups, partials, base_parts, up_cores, pieces
    )

    base = [send(partials[m - 1], flips[m]) for m in (1, 2)]
    while len(downs) < planes:
        downs.append(send(downs[-1], ring))
    ups.append(send(ups[0], ring))
    last, own = base_products([far, message], base_parts, spots, [jnp.bfloat16, jnp.float32])
    pieces = pieces + sum([both(d) for d in downs[2:-1]], [])
    base, downs, ups, last, own, pieces, up_cores = phase(
        base, downs, ups, last, own, pieces, up_cores
    )

    base = [own, *base, send(last, flips[3])]
    blocks = [message, *near, far]
    pieces = pieces + both(downs[-1])
    for k in range(2, planes):
        after_k = {order[i]: order[(i + k) % planes] for i in range(planes)}
        pairs = []
        for a, b in everyone:
            to = after_k[b // (2 * sides)] * 2 * sides + b % (2 * sides)
            pairs.append((a * peers + b, a * peers + to))
        ups.append(send(ups[0], pairs))
    first = rows + dec
    packed = lowered_products(blocks, pieces, columns, rows, first, rank, last)
    _, ups = phase(packed, ups)
    packed = [packed[0]] + [send(packed[m], flips[m]) for m in (1, 2, 3)]
    up_parts = ups + up_cores + [send(u, cores) for u in ups[1:]]
    base, packed, up_parts = phase(base, packed, up_parts)
    return tuple(
        finish(
            packed,
            message,
            up_parts,
            up_columns,
            base,
            rows,
            first,
            rank,
            cached,
            dec,
        )
    )


def solution(mesh):
    in_specs = (
        P(BOTH, None),
        P(BOTH, None),
        P(),
        P(BOTH, None),
        P(BOTH, None),
        P(BOTH, None, None),
        P(BOTH, None, None),
        P(BOTH),
        P("tenant", None),
        P("tenant", None, None),
        P("tenant", None, None),
    )
    out_specs = (P(BOTH, None), P(BOTH, None))
    return jax.shard_map(body, mesh=mesh, in_specs=in_specs, out_specs=out_specs, check_vma=False)
```

```python
import math

import jax
import jax.numpy as jnp
from jax import lax
from jax.experimental import pallas as pl
from jax.experimental.pallas import tpu as pltpu
from jax.sharding import PartitionSpec as P

HEAD_SIZE = 128
adapter_scale = 2.0
VMEM = 60 * 2**20
BOTH = ("replica", "tenant")


def cost(flops, bytes_accessed):
    return pl.CostEstimate(flops=flops, bytes_accessed=bytes_accessed, transcendentals=0)


def cost(flops, bytes_accessed):
    return pl.CostEstimate(flops=flops, bytes_accessed=bytes_accessed, transcendentals=0)


def column_spot(rep, y, m, j, reps, sides):
    other = (y * reps + rep) ^ m
    return ((j // 2 * sides + other // reps) * 2 + j % 2) * reps + other % reps


def split_down(down, place, steps, kk, reps, sides, flips):
    ranks = down.shape[0]
    wide = steps * kk
    if kk % 128:

        def pick(m):
            cut = down.reshape(ranks, -1, kk)
            order = jnp.arange(steps, dtype=jnp.int32)
            order = column_spot(place[0], place[1], m, order, reps, sides)
            return jnp.take(cut, order, axis=1).reshape(ranks, wide)

        return [pick(m) for m in flips]

    def kernel(here, dwn, *outs):
        for i, m in enumerate(flips):
            for j in range(steps):
                at = column_spot(here[0], here[1], m, j, reps, sides)
                outs[i][:, j * kk : (j + 1) * kk] = dwn[:, pl.ds(pl.multiple_of(at * kk, kk), kk)]

    whole = lambda j, *_: (0, 0)
    return pl.pallas_call(
        kernel,
        grid_spec=pltpu.PrefetchScalarGridSpec(
            num_scalar_prefetch=1,
            grid=(1,),
            in_specs=[pl.BlockSpec(down.shape, whole)],
            out_specs=[pl.BlockSpec((ranks, wide), whole)] * len(flips),
        ),
        out_shape=[jax.ShapeDtypeStruct((ranks, wide), jnp.bfloat16)] * len(flips),
        compiler_params=pltpu.CompilerParams(vmem_limit_bytes=VMEM),
        cost_estimate=cost(0, 2 * 2**20),
        name="split_down",
    )(place, down)


def split_columns(prefill, decode, tenants, owner, place, steps, kk, reps, sides, pad):
    rows, dec = prefill.shape[0], decode.shape[0]
    wide = steps * kk
    slots_all = owner.shape[0]
    if kk % 128:
        stacked = jnp.concatenate([prefill, decode], axis=0)
        hot = tenants.reshape(rows, 1) == jnp.arange(slots_all, dtype=jnp.int32)[None, :]
        slots = jnp.sum(jnp.where(hot, owner[None, :], 0), axis=1).astype(jnp.bfloat16)
        slots = jnp.broadcast_to(jnp.pad(slots, (0, wide - rows))[None, :], (pad, wide))

        def pick(m):
            cut = stacked.reshape(stacked.shape[0], -1, kk)
            order = jnp.arange(steps, dtype=jnp.int32)
            order = column_spot(place[0], place[1], m, order, reps, sides)
            return jnp.take(cut, order, axis=1).reshape(stacked.shape[0], wide)

        return [jnp.concatenate([pick(m), slots], axis=0) for m in range(4)]
    turns = 2
    each = steps // turns

    def kernel(here, own, pre, dcd, ten, *outs):
        turn = pl.program_id(0)
        slot = jnp.zeros((1, rows), jnp.float32)
        for s in range(slots_all):
            slot = jnp.where(ten[...] == s, own[s].astype(jnp.float32), slot)
        slot = jnp.broadcast_to(slot, (pad, rows)).astype(jnp.bfloat16)
        slot = jnp.concatenate([slot] + [jnp.zeros_like(slot)] * (each * kk // rows - 1), axis=1)
        for m in range(4):
            for i in range(each):
                at = column_spot(here[0], here[1], m, turn * each + i, reps, sides)
                at = pl.ds(pl.multiple_of(at * kk, kk), kk)
                to = slice(i * kk, (i + 1) * kk)
                outs[m][0:rows, to] = pre[:, at]
                below = jnp.concatenate([dcd[:, at], slot[:, to]], axis=0)
                outs[m][rows : rows + dec + pad, to] = below

    out = lambda j, *_: (0, j)
    whole = lambda j, *_: (0, 0)
    return pl.pallas_call(
        kernel,
        grid_spec=pltpu.PrefetchScalarGridSpec(
            num_scalar_prefetch=2,
            grid=(turns,),
            in_specs=[pl.BlockSpec(a.shape, whole) for a in (prefill, decode, tenants)],
            out_specs=[pl.BlockSpec((rows + dec + pad, each * kk), out)] * 4,
        ),
        out_shape=[jax.ShapeDtypeStruct((rows + dec + pad, wide), jnp.bfloat16)] * 4,
        compiler_params=pltpu.CompilerParams(vmem_limit_bytes=VMEM),
        cost_estimate=cost(0, 9 * 2**20),
        name="split_columns",
    )(place, owner, prefill, decode, tenants)


def base_products(blocks, parts, spots, kinds):
    kk, out_width = parts[0].shape
    tall = blocks[0].shape[0]
    n = len(parts)
    if kk % 128:
        quarter = jnp.zeros((n * kk, out_width), jnp.bfloat16)
        for i in range(n):
            quarter = lax.dynamic_update_slice_in_dim(quarter, parts[i], spots[i] * kk, axis=0)
        products = [jnp.dot(b, quarter, preferred_element_type=jnp.float32) for b in blocks]
        return [p.astype(kind) for p, kind in zip(products, kinds)]
    count = len(blocks)
    cut = 256

    def kernel(spot, *refs):
        xs, weights = refs[:count], refs[count : count + n]
        outs = refs[count + n : 2 * count + n]
        left, right = refs[-2:]

        @pl.when(pl.program_id(0) == 0)
        def _():
            for m in range(count):
                left[m * tall : (m + 1) * tall] = xs[m][...]

        for i in range(n):
            right[pl.ds(pl.multiple_of(spot[i] * kk, kk), kk), :] = weights[i][...]
        total = jnp.dot(left[...], right[...], preferred_element_type=jnp.float32)
        for m in range(count):
            outs[m][...] = total[m * tall : (m + 1) * tall].astype(kinds[m])

    outs = pl.pallas_call(
        kernel,
        grid_spec=pltpu.PrefetchScalarGridSpec(
            num_scalar_prefetch=1,
            grid=(out_width // cut,),
            in_specs=[pl.BlockSpec(blocks[0].shape, lambda j, s: (0, 0))] * count
            + [pl.BlockSpec((kk, cut), lambda j, s: (0, j))] * n,
            out_specs=[pl.BlockSpec((tall, cut), lambda j, s: (0, j))] * count,
            scratch_shapes=[
                pltpu.VMEM((count * tall, n * kk), jnp.bfloat16),
                pltpu.VMEM((n * kk, cut), jnp.bfloat16),
            ],
        ),
        out_shape=[jax.ShapeDtypeStruct((tall, out_width), kind) for kind in kinds],
        compiler_params=pltpu.CompilerParams(vmem_limit_bytes=28 * 2**20),
        cost_estimate=cost(2 * count * tall * n * kk * out_width, (count * tall + out_width) * 2 * n * kk),
        name="base_products",
    )(spots, *blocks, *parts)
    return list(outs)


def lowered_products(blocks, pieces, columns, rows, first, rank, after):
    wide = blocks[0].shape[1]
    ranks = pieces[0].shape[0]
    total_ranks = len(pieces) * ranks
    count = len(blocks)
    folds = 128 // rank
    n = len(pieces)
    tall = rows // folds
    if n > 16:
        sums = []
        down = jnp.concatenate(pieces, axis=0)
        for b in blocks:
            product = lax.dot_general(
                b[:rows], down, (((1,), (1,)), ((), ())), preferred_element_type=jnp.float32
            )
            slot = b[first, :rows].astype(jnp.float32)
            kept = jnp.where(slot[:, None] == columns, product, 0.0)
            kept = sum(kept[:, i : i + rank] for i in range(0, total_ranks, rank))
            sums.append(jnp.concatenate(jnp.split(kept, folds, axis=0), axis=1))
        return sums
    base_row = first // 16 * 16

    def kernel(_, *refs):
        xs, ds = refs[:count], refs[count : count + n]
        col, outs, left = refs[count + n], refs[count + n + 1 : -1], refs[-1]
        slot = []
        for m in range(count):
            left[m * rows : (m + 1) * rows] = xs[m][:rows]
            slot.append(xs[m][base_row : base_row + 16, :rows].astype(jnp.float32))
        slot = [jnp.transpose(s)[:, first - base_row : first - base_row + 1] for s in slot]
        slot = jnp.broadcast_to(jnp.concatenate(slot, axis=0), (count * rows, 128))
        kept = None
        for i in range(0, n, 2):
            down = jnp.concatenate([d[...] for d in ds[i : i + 2]], axis=0)
            term = lax.dot_general(
                left[...], down, (((1,), (1,)), ((), ())), preferred_element_type=jnp.float32
            )
            for h in range(0, 2 * ranks, 128):
                at = i * ranks + h
                part = jnp.where(slot == col[0:1, at : at + 128], term[:, h : h + 128], 0.0)
                kept = part if kept is None else kept + part
        kept = kept + pltpu.roll(kept, rank, 1)
        kept = kept + pltpu.roll(kept, 2 * rank, 1)
        lane = lax.broadcasted_iota(jnp.int32, (tall, 128), 1) // rank
        for m in range(count):
            packed = jnp.zeros((tall, 128), jnp.float32)
            for b in range(folds):
                at = m * rows + b * tall
                packed = jnp.where(lane == b, kept[at : at + tall], packed)
            outs[m][...] = packed

    whole = lambda j: (0, 0)
    return pl.pallas_call(
        kernel,
        grid=(1,),
        in_specs=[pl.BlockSpec(memory_space=pl.ANY)]
        + [pl.BlockSpec(blocks[0].shape, whole)] * count
        + [pl.BlockSpec((ranks, wide), whole)] * n
        + [pl.BlockSpec(columns.shape, whole)],
        out_specs=[pl.BlockSpec((tall, 128), whole)] * count,
        out_shape=[jax.ShapeDtypeStruct((tall, 128), jnp.float32)] * count,
        scratch_shapes=[pltpu.VMEM((count * rows, wide), jnp.bfloat16)],
        compiler_params=pltpu.CompilerParams(vmem_limit_bytes=32 * 2**20),
        cost_estimate=cost(2 * count * rows * wide * total_ranks, (count * rows + total_ranks) * 2 * wide),
        name="lowered_products",
    )(after, *blocks, *pieces, columns)


def own_attention(fresh, queries, tops, totals, mix):
    dec, out_width = fresh.shape
    heads = queries.shape[0] // dec
    kv_heads = out_width // 2 // HEAD_SIZE
    fresh = fresh.astype(jnp.bfloat16).astype(jnp.float32)
    parts = [fresh[:, i * HEAD_SIZE : (i + 1) * HEAD_SIZE] for i in range(2 * kv_heads)]
    group = heads // kv_heads
    keys = jnp.concatenate([parts[h // group] for h in range(heads)], axis=0)
    values = jnp.concatenate([parts[kv_heads + h // group] for h in range(heads)], axis=0)
    own = jnp.sum(queries.astype(jnp.float32) * keys, axis=1, keepdims=True)
    own = jnp.broadcast_to(own * (1.0 / math.sqrt(HEAD_SIZE)), mix.shape)
    tops, totals = jnp.broadcast_to(tops, mix.shape), jnp.broadcast_to(totals, mix.shape)
    top = jnp.maximum(tops, own)
    kept, weight = jnp.exp(tops - top), jnp.exp(own - top)
    mixed = (kept * mix + weight * values) / (kept * totals + weight)
    mixed = mixed.astype(jnp.bfloat16)
    return [mixed[h * dec : (h + 1) * dec] for h in range(heads)]


def finish(parts, block, ups, columns, bases, rows, first, rank, cached, dec):
    heads = cached[0].shape[0] // dec
    shape = (dec, heads * HEAD_SIZE)
    packed_rows = parts[0].shape[0]
    folds = rows // packed_rows
    out_width = bases[0].shape[1]
    n = len(ups)
    tall = ups[0].shape[0]
    base_row = first // 16 * 16
    if n * tall > 2048:
        lowered = sum(parts[1:], parts[0]).astype(jnp.bfloat16)
        lowered = jnp.concatenate(
            [lowered[:, b * rank : (b + 1) * rank] for b in range(folds)], axis=0
        )
        slot = block[first, :rows].astype(jnp.float32)
        spread = jnp.where(
            slot[:, None] == columns, jnp.tile(lowered, (1, n * tall // rank)), jnp.bfloat16(0)
        )
        up = jnp.concatenate(ups, axis=0)
        delta = jnp.dot(spread, up, preferred_element_type=jnp.float32).astype(jnp.bfloat16)
        base = sum(b.astype(jnp.float32) for b in bases)
        attended = own_attention(base[rows : rows + dec], *cached)
        base = base[:rows]
        projected = (base + adapter_scale * delta.astype(jnp.float32)).astype(jnp.bfloat16)
        return projected, jnp.concatenate(attended, axis=1)
    cut = 256
    below = bases[0].shape[0] - rows

    def kernel(*refs):
        packs = refs[:4]
        blk, col = refs[4:6]
        bas, upr = refs[6:10], refs[10 : 10 + n]
        own, old = refs[10 + n : 14 + n], refs[14 + n : 18 + n]
        out, out_attended, wide = refs[18 + n :]

        @pl.when(pl.program_id(0) == 0)
        def _():
            slot = jnp.transpose(blk[...].astype(jnp.float32))
            slot = slot[:, first - base_row : first - base_row + 1]
            packed = (packs[0][...] + packs[1][...]) + (packs[2][...] + packs[3][...])
            lane = lax.broadcasted_iota(jnp.int32, packed.shape, 1) // rank
            spread = []
            for b in range(folds):
                one = jnp.where(lane == b, packed, 0.0)
                one = one + pltpu.roll(one, rank, 1)
                one = one + pltpu.roll(one, 2 * rank, 1)
                spread.append(one)
            lowered = jnp.concatenate(spread, axis=0)
            for i in range(0, n * tall, 128):
                kept = jnp.where(slot == col[0:1, i : i + 128], lowered, 0.0)
                wide[:, i : i + 128] = kept.astype(jnp.bfloat16)
            fresh = own[0][...]
            for b in own[1:]:
                fresh = fresh + b[...].astype(jnp.float32)
            parts_own = own_attention(fresh[:dec], *[c[...] for c in old])
            for h in range(heads):
                out_attended[:, h * HEAD_SIZE : (h + 1) * HEAD_SIZE] = parts_own[h]

        up = jnp.concatenate([u[...] for u in upr], axis=0)
        delta = jnp.dot(wide[...], up, preferred_element_type=jnp.float32)
        base = bas[0][0:rows]
        for b in bas[1:]:
            base = base + b[0:rows].astype(jnp.float32)
        out[...] = (base + adapter_scale * delta.astype(jnp.bfloat16).astype(jnp.float32)).astype(
            jnp.bfloat16
        )

    one = lambda j: (0, 0)
    column = lambda j: (0, j)
    return pl.pallas_call(
        kernel,
        grid=(out_width // cut,),
        in_specs=[pl.BlockSpec(parts[0].shape, one)] * 4
        + [
            pl.BlockSpec((16, rows), lambda j: (base_row // 16, 0)),
            pl.BlockSpec(columns.shape, one),
        ]
        + [pl.BlockSpec((bases[0].shape[0], cut), column)] * 4
        + [pl.BlockSpec((tall, cut), column)] * n
        + [pl.BlockSpec((below, out_width), lambda j: (rows // below, 0))] * 4
        + [pl.BlockSpec(a.shape, one) for a in cached],
        out_specs=[pl.BlockSpec((rows, cut), column), pl.BlockSpec(shape, one)],
        out_shape=[
            jax.ShapeDtypeStruct((rows, out_width), jnp.bfloat16),
            jax.ShapeDtypeStruct(shape, jnp.bfloat16),
        ],
        scratch_shapes=[pltpu.VMEM((rows, n * tall), jnp.bfloat16)],
        compiler_params=pltpu.CompilerParams(vmem_limit_bytes=VMEM),
        cost_estimate=cost(2 * rows * n * tall * out_width, 5 * 2**20),
        name="finish",
    )(*parts, block, columns, *bases, *ups, *bases, *cached)


def body(
    prefill_rows,
    tenant_ids,
    owner_slot,
    decode_rows,
    queries,
    key_store_cache,
    value_store_cache,
    context_len,
    base_weight,
    adapter_down,
    adapter_up,
):
    reps, peers = lax.axis_size("replica"), lax.axis_size("tenant")
    planes = reps * peers // 8
    sides = peers // (2 * planes)
    local_slots, rank, width = adapter_down.shape
    slots_all = local_slots * peers
    rows, dec = prefill_rows.shape[0], decode_rows.shape[0]
    out_width = base_weight.shape[1]
    half_width = out_width // 2
    kk = base_weight.shape[0] // reps
    steps = 2 * planes
    quarter = steps * kk
    pad = 16 - dec % 16
    r, t = lax.axis_index("replica"), lax.axis_index("tenant")
    z, y, c = t // (2 * sides), (t // 2) % sides, t % 2
    q = y * reps + r

    order = list(range(0, planes, 2)) + list(range(1, planes, 2))[::-1]
    after = {order[i]: order[(i + 1) % planes] for i in range(planes)}
    everyone = [(a, b) for a in range(reps) for b in range(peers)]

    def flip(m):
        pairs = []
        for a, b in everyone:
            other = (((b // 2) % sides) * reps + a) ^ m
            to = (b // (2 * sides) * sides + other // reps) * 2 + b % 2
            pairs.append((a * peers + b, (other % reps) * peers + to))
        return pairs

    flips = {m: flip(m) for m in (1, 2, 3)}
    ring = [
        (a * peers + b, a * peers + after[b // (2 * sides)] * 2 * sides + b % (2 * sides))
        for a, b in everyone
    ]
    cores = [(a * peers + b, a * peers + (b ^ 1)) for a, b in everyone]

    def send(value, pairs):
        return lax.ppermute(value, BOTH, pairs)

    place = jnp.where(z % 2 == 0, z // 2, planes - 1 - z // 2)

    def plane_of(k):
        spot = (place - k + planes) % planes
        return jnp.where(spot < planes // 2, 2 * spot, 2 * (planes - 1 - spot) + 1)

    spots = jnp.arange(steps, dtype=jnp.int32)
    spots = plane_of(spots // 2) * 2 + (c ^ (spots % 2))
    ranks = local_slots * rank

    def both(value):
        return [value, send(value, cores)]

    def phase(*values):
        return lax.optimization_barrier(values)

    def paired(near, far):
        return near if far is None else jnp.concatenate([near, far], axis=0)

    bases = [lax.dynamic_slice_in_dim(base_weight, r * kk, kk, axis=0)]
    up = adapter_up.reshape(ranks, out_width)
    here, bases, up = phase(jnp.stack([r, y]), bases, up)
    bases.append(send(bases[0], ring))
    up_far = send(up, flips[reps]) if sides == 2 else None
    y_flips = [0, reps] if sides == 2 else [0]
    downs = split_down(adapter_down.reshape(ranks, width), here, steps, kk, reps, sides, y_flips)
    here, downs = phase(here, downs)
    down_far = send(downs[1], flips[reps]) if sides == 2 else None
    messages = split_columns(
        prefill_rows,
        decode_rows,
        tenant_ids.reshape(1, rows),
        owner_slot,
        here,
        steps,
        kk,
        reps,
        sides,
        pad,
    )
    downs = [paired(downs[0], down_far)]
    ups = [paired(up, up_far)]
    base_parts = both(bases[0])
    bases, downs, ups, messages, base_parts = phase(bases, downs, ups, messages, base_parts)
    near = [send(messages[m], flips[m]) for m in (1, 2)]
    message = messages[0]

    bases.append(send(bases[-1], ring))
    bases, queries = phase(bases, queries)
    while len(bases) < planes:
        bases.append(send(bases[-1], ring))
    for held in bases[1:2]:
        base_parts = base_parts + both(held)

    kv_heads = half_width // HEAD_SIZE
    query_groups = queries.shape[1] // half_width
    positions = key_store_cache.shape[1]
    query_head_rows = queries.reshape(dec, kv_heads, query_groups, HEAD_SIZE)
    stored_keys = key_store_cache.reshape(dec, positions, kv_heads, HEAD_SIZE)
    stored_values = value_store_cache.reshape(dec, positions, kv_heads, HEAD_SIZE)
    scale = 1.0 / math.sqrt(HEAD_SIZE)
    scores = (
        jnp.einsum(
            "bkgd,bckd->bkgc", query_head_rows, stored_keys, preferred_element_type=jnp.float32
        )
        * scale
    )
    live = jnp.arange(positions, dtype=jnp.int32)[None, :] < context_len[:, None]
    scores = jnp.where(live[:, None, None, :], scores, -jnp.inf)
    cached_top = jnp.max(scores, axis=-1)
    cached_weight = jnp.exp(scores - cached_top[..., None])
    cached_total = jnp.sum(cached_weight, axis=-1)
    cached_mix = jnp.einsum(
        "bkgc,bckd->bkgd",
        cached_weight.astype(jnp.bfloat16),
        stored_values,
        preferred_element_type=jnp.float32,
    )
    tall = kv_heads * query_groups * dec

    def by_head(value):
        value = value if value.ndim == 4 else value[..., None]
        return value.transpose(1, 2, 0, 3).reshape(tall, value.shape[3])

    cached = [by_head(v) for v in (query_head_rows, cached_top, cached_total, cached_mix)]

    group = jnp.arange(slots_all, dtype=jnp.int32)
    inner = group % local_slots
    side = (group // local_slots) % sides
    core = (group // (local_slots * sides)) % 2
    step = group // (local_slots * sides * 2)
    column_slot = ((plane_of(step) * sides + (y ^ side)) * 2 + (c ^ core)) * local_slots + inner
    columns = jnp.repeat(column_slot, rank).astype(jnp.float32)[None, :]
    core = group // (local_slots * sides * planes)
    step = (group // (local_slots * sides)) % planes
    column_slot = ((plane_of(step) * sides + (y ^ side)) * 2 + (c ^ core)) * local_slots + inner
    up_columns = jnp.repeat(column_slot, rank).astype(jnp.float32)[None, :]

    pieces = both(downs[0])
    near, bases, ups, far, base_parts, pieces, cached, columns, up_columns, spots = phase(
        near, bases, ups, messages[3], base_parts, pieces, cached, columns, up_columns, spots
    )

    far = send(far, flips[3])
    while len(downs) < max(2, planes - 1):
        downs.append(send(downs[-1], ring))
    for held in bases[2:]:
        base_parts = base_parts + both(held)
    partials = base_products(near, base_parts, spots, [jnp.bfloat16] * 2)
    up_cores = [send(ups[0], cores)]
    pieces = pieces + both(downs[1])
    far, downs, ups, partials, base_parts, up_cores, pieces = phase(
        far, downs, ups, partials, base_parts, up_cores, pieces
    )

    base = [send(partials[m - 1], flips[m]) for m in (1, 2)]
    while len(downs) < planes:
        downs.append(send(downs[-1], ring))
    ups.append(send(ups[0], ring))
    last, own = base_products([far, message], base_parts, spots, [jnp.bfloat16, jnp.float32])
    pieces = pieces + sum([both(d) for d in downs[2:-1]], [])
    base, downs, ups, last, own, pieces, up_cores = phase(
        base, downs, ups, last, own, pieces, up_cores
    )

    base = [own, *base, send(last, flips[3])]
    blocks = [message, *near, far]
    pieces = pieces + both(downs[-1])
    for k in range(2, planes):
        after_k = {order[i]: order[(i + k) % planes] for i in range(planes)}
        pairs = []
        for a, b in everyone:
            to = after_k[b // (2 * sides)] * 2 * sides + b % (2 * sides)
            pairs.append((a * peers + b, a * peers + to))
        ups.append(send(ups[0], pairs))
    first = rows + dec
    packed = lowered_products(blocks, pieces, columns, rows, first, rank, last)
    packed = [packed[0]] + [send(packed[m], flips[m]) for m in (1, 2, 3)]
    packed, ups = phase(packed, ups)
    up_parts = ups + up_cores + [send(u, cores) for u in ups[1:]]
    base, packed, up_parts = phase(base, packed, up_parts)
    return tuple(
        finish(
            packed,
            message,
            up_parts,
            up_columns,
            base,
            rows,
            first,
            rank,
            cached,
            dec,
        )
    )


def solution(mesh):
    in_specs = (
        P(BOTH, None),
        P(BOTH, None),
        P(),
        P(BOTH, None),
        P(BOTH, None),
        P(BOTH, None, None),
        P(BOTH, None, None),
        P(BOTH),
        P("tenant", None),
        P("tenant", None, None),
        P("tenant", None, None),
    )
    out_specs = (P(BOTH, None), P(BOTH, None))
    return jax.shard_map(body, mesh=mesh, in_specs=in_specs, out_specs=out_specs, check_vma=False)
```

```python
import math

import jax
import jax.numpy as jnp
from jax import lax
from jax.experimental import pallas as pl
from jax.experimental.pallas import tpu as pltpu
from jax.sharding import PartitionSpec as P

HEAD_SIZE = 128
adapter_scale = 2.0
VMEM = 60 * 2**20
BOTH = ("replica", "tenant")


def cost(flops, bytes_accessed):
    return pl.CostEstimate(flops=flops, bytes_accessed=bytes_accessed, transcendentals=0)


def cost(flops, bytes_accessed):
    return pl.CostEstimate(flops=flops, bytes_accessed=bytes_accessed, transcendentals=0)


def column_spot(rep, y, m, j, reps, sides):
    other = (y * reps + rep) ^ m
    return ((j // 2 * sides + other // reps) * 2 + j % 2) * reps + other % reps


def split_down(down, place, steps, kk, reps, sides, flips):
    ranks = down.shape[0]
    wide = steps * kk
    if kk % 128:

        def pick(m):
            cut = down.reshape(ranks, -1, kk)
            order = jnp.arange(steps, dtype=jnp.int32)
            order = column_spot(place[0], place[1], m, order, reps, sides)
            return jnp.take(cut, order, axis=1).reshape(ranks, wide)

        return [pick(m) for m in flips]

    def kernel(here, dwn, *outs):
        for i, m in enumerate(flips):
            for j in range(steps):
                at = column_spot(here[0], here[1], m, j, reps, sides)
                outs[i][:, j * kk : (j + 1) * kk] = dwn[:, pl.ds(pl.multiple_of(at * kk, kk), kk)]

    whole = lambda j, *_: (0, 0)
    return pl.pallas_call(
        kernel,
        grid_spec=pltpu.PrefetchScalarGridSpec(
            num_scalar_prefetch=1,
            grid=(1,),
            in_specs=[pl.BlockSpec(down.shape, whole)],
            out_specs=[pl.BlockSpec((ranks, wide), whole)] * len(flips),
        ),
        out_shape=[jax.ShapeDtypeStruct((ranks, wide), jnp.bfloat16)] * len(flips),
        compiler_params=pltpu.CompilerParams(vmem_limit_bytes=VMEM),
        cost_estimate=cost(0, 2 * 2**20),
        name="split_down",
    )(place, down)


def split_columns(prefill, decode, tenants, owner, place, steps, kk, reps, sides, pad):
    rows, dec = prefill.shape[0], decode.shape[0]
    wide = steps * kk
    slots_all = owner.shape[0]
    if kk % 128:
        stacked = jnp.concatenate([prefill, decode], axis=0)
        hot = tenants.reshape(rows, 1) == jnp.arange(slots_all, dtype=jnp.int32)[None, :]
        slots = jnp.sum(jnp.where(hot, owner[None, :], 0), axis=1).astype(jnp.bfloat16)
        slots = jnp.broadcast_to(jnp.pad(slots, (0, wide - rows))[None, :], (pad, wide))

        def pick(m):
            cut = stacked.reshape(stacked.shape[0], -1, kk)
            order = jnp.arange(steps, dtype=jnp.int32)
            order = column_spot(place[0], place[1], m, order, reps, sides)
            return jnp.take(cut, order, axis=1).reshape(stacked.shape[0], wide)

        return [jnp.concatenate([pick(m), slots], axis=0) for m in range(4)]
    turns = 2
    each = steps // turns

    def kernel(here, own, pre, dcd, ten, *outs):
        turn = pl.program_id(0)
        slot = jnp.zeros((1, rows), jnp.float32)
        for s in range(slots_all):
            slot = jnp.where(ten[...] == s, own[s].astype(jnp.float32), slot)
        slot = jnp.broadcast_to(slot, (pad, rows)).astype(jnp.bfloat16)
        slot = jnp.concatenate([slot] + [jnp.zeros_like(slot)] * (each * kk // rows - 1), axis=1)
        for m in range(4):
            for i in range(each):
                at = column_spot(here[0], here[1], m, turn * each + i, reps, sides)
                at = pl.ds(pl.multiple_of(at * kk, kk), kk)
                to = slice(i * kk, (i + 1) * kk)
                outs[m][0:rows, to] = pre[:, at]
                below = jnp.concatenate([dcd[:, at], slot[:, to]], axis=0)
                outs[m][rows : rows + dec + pad, to] = below

    out = lambda j, *_: (0, j)
    whole = lambda j, *_: (0, 0)
    return pl.pallas_call(
        kernel,
        grid_spec=pltpu.PrefetchScalarGridSpec(
            num_scalar_prefetch=2,
            grid=(turns,),
            in_specs=[pl.BlockSpec(a.shape, whole) for a in (prefill, decode, tenants)],
            out_specs=[pl.BlockSpec((rows + dec + pad, each * kk), out)] * 4,
        ),
        out_shape=[jax.ShapeDtypeStruct((rows + dec + pad, wide), jnp.bfloat16)] * 4,
        compiler_params=pltpu.CompilerParams(vmem_limit_bytes=VMEM),
        cost_estimate=cost(0, 9 * 2**20),
        name="split_columns",
    )(place, owner, prefill, decode, tenants)


def base_products(blocks, parts, spots, kinds):
    kk, out_width = parts[0].shape
    tall = blocks[0].shape[0]
    n = len(parts)
    if kk % 128:
        quarter = jnp.zeros((n * kk, out_width), jnp.bfloat16)
        for i in range(n):
            quarter = lax.dynamic_update_slice_in_dim(quarter, parts[i], spots[i] * kk, axis=0)
        products = [jnp.dot(b, quarter, preferred_element_type=jnp.float32) for b in blocks]
        return [p.astype(kind) for p, kind in zip(products, kinds)]
    count = len(blocks)
    cut = 256

    def kernel(spot, *refs):
        xs, weights = refs[:count], refs[count : count + n]
        outs = refs[count + n : 2 * count + n]
        left, right = refs[-2:]

        @pl.when(pl.program_id(0) == 0)
        def _():
            for m in range(count):
                left[m * tall : (m + 1) * tall] = xs[m][...]

        for i in range(n):
            right[pl.ds(pl.multiple_of(spot[i] * kk, kk), kk), :] = weights[i][...]
        total = jnp.dot(left[...], right[...], preferred_element_type=jnp.float32)
        for m in range(count):
            outs[m][...] = total[m * tall : (m + 1) * tall].astype(kinds[m])

    outs = pl.pallas_call(
        kernel,
        grid_spec=pltpu.PrefetchScalarGridSpec(
            num_scalar_prefetch=1,
            grid=(out_width // cut,),
            in_specs=[pl.BlockSpec(blocks[0].shape, lambda j, s: (0, 0))] * count
            + [pl.BlockSpec((kk, cut), lambda j, s: (0, j))] * n,
            out_specs=[pl.BlockSpec((tall, cut), lambda j, s: (0, j))] * count,
            scratch_shapes=[
                pltpu.VMEM((count * tall, n * kk), jnp.bfloat16),
                pltpu.VMEM((n * kk, cut), jnp.bfloat16),
            ],
        ),
        out_shape=[jax.ShapeDtypeStruct((tall, out_width), kind) for kind in kinds],
        compiler_params=pltpu.CompilerParams(vmem_limit_bytes=28 * 2**20),
        cost_estimate=cost(2 * count * tall * n * kk * out_width, (count * tall + out_width) * 2 * n * kk),
        name="base_products",
    )(spots, *blocks, *parts)
    return list(outs)


def lowered_products(blocks, pieces, columns, rows, first, rank, after):
    wide = blocks[0].shape[1]
    ranks = pieces[0].shape[0]
    total_ranks = len(pieces) * ranks
    count = len(blocks)
    folds = 128 // rank
    n = len(pieces)
    tall = rows // folds
    if n > 16:
        sums = []
        down = jnp.concatenate(pieces, axis=0)
        for b in blocks:
            product = lax.dot_general(
                b[:rows], down, (((1,), (1,)), ((), ())), preferred_element_type=jnp.float32
            )
            slot = b[first, :rows].astype(jnp.float32)
            kept = jnp.where(slot[:, None] == columns, product, 0.0)
            kept = sum(kept[:, i : i + rank] for i in range(0, total_ranks, rank))
            sums.append(jnp.concatenate(jnp.split(kept, folds, axis=0), axis=1))
        return sums
    base_row = first // 16 * 16

    def kernel(_, *refs):
        xs, ds = refs[:count], refs[count : count + n]
        col, outs, left = refs[count + n], refs[count + n + 1 : -1], refs[-1]
        slot = []
        for m in range(count):
            left[m * rows : (m + 1) * rows] = xs[m][:rows]
            slot.append(xs[m][base_row : base_row + 16, :rows].astype(jnp.float32))
        slot = [jnp.transpose(s)[:, first - base_row : first - base_row + 1] for s in slot]
        slot = jnp.broadcast_to(jnp.concatenate(slot, axis=0), (count * rows, 128))
        kept = None
        for i in range(0, n, 2):
            down = jnp.concatenate([d[...] for d in ds[i : i + 2]], axis=0)
            term = lax.dot_general(
                left[...], down, (((1,), (1,)), ((), ())), preferred_element_type=jnp.float32
            )
            for h in range(0, 2 * ranks, 128):
                at = i * ranks + h
                part = jnp.where(slot == col[0:1, at : at + 128], term[:, h : h + 128], 0.0)
                kept = part if kept is None else kept + part
        kept = kept + pltpu.roll(kept, rank, 1)
        kept = kept + pltpu.roll(kept, 2 * rank, 1)
        lane = lax.broadcasted_iota(jnp.int32, (tall, 128), 1) // rank
        for m in range(count):
            packed = jnp.zeros((tall, 128), jnp.float32)
            for b in range(folds):
                at = m * rows + b * tall
                packed = jnp.where(lane == b, kept[at : at + tall], packed)
            outs[m][...] = packed

    whole = lambda j: (0, 0)
    return pl.pallas_call(
        kernel,
        grid=(1,),
        in_specs=[pl.BlockSpec(memory_space=pl.ANY)]
        + [pl.BlockSpec(blocks[0].shape, whole)] * count
        + [pl.BlockSpec((ranks, wide), whole)] * n
        + [pl.BlockSpec(columns.shape, whole)],
        out_specs=[pl.BlockSpec((tall, 128), whole)] * count,
        out_shape=[jax.ShapeDtypeStruct((tall, 128), jnp.float32)] * count,
        scratch_shapes=[pltpu.VMEM((count * rows, wide), jnp.bfloat16)],
        compiler_params=pltpu.CompilerParams(vmem_limit_bytes=32 * 2**20),
        cost_estimate=cost(2 * count * rows * wide * total_ranks, (count * rows + total_ranks) * 2 * wide),
        name="lowered_products",
    )(after, *blocks, *pieces, columns)


def own_attention(fresh, queries, tops, totals, mix):
    dec, out_width = fresh.shape
    heads = queries.shape[0] // dec
    kv_heads = out_width // 2 // HEAD_SIZE
    fresh = fresh.astype(jnp.bfloat16).astype(jnp.float32)
    parts = [fresh[:, i * HEAD_SIZE : (i + 1) * HEAD_SIZE] for i in range(2 * kv_heads)]
    group = heads // kv_heads
    keys = jnp.concatenate([parts[h // group] for h in range(heads)], axis=0)
    values = jnp.concatenate([parts[kv_heads + h // group] for h in range(heads)], axis=0)
    own = jnp.sum(queries.astype(jnp.float32) * keys, axis=1, keepdims=True)
    own = jnp.broadcast_to(own * (1.0 / math.sqrt(HEAD_SIZE)), mix.shape)
    tops, totals = jnp.broadcast_to(tops, mix.shape), jnp.broadcast_to(totals, mix.shape)
    top = jnp.maximum(tops, own)
    kept, weight = jnp.exp(tops - top), jnp.exp(own - top)
    mixed = (kept * mix + weight * values) / (kept * totals + weight)
    mixed = mixed.astype(jnp.bfloat16)
    return [mixed[h * dec : (h + 1) * dec] for h in range(heads)]


def finish(parts, block, ups, columns, bases, rows, first, rank, cached, dec):
    heads = cached[0].shape[0] // dec
    shape = (dec, heads * HEAD_SIZE)
    packed_rows = parts[0].shape[0]
    folds = rows // packed_rows
    out_width = bases[0].shape[1]
    n = len(ups)
    tall = ups[0].shape[0]
    base_row = first // 16 * 16
    if n * tall > 2048:
        lowered = sum(parts[1:], parts[0]).astype(jnp.bfloat16)
        lowered = jnp.concatenate(
            [lowered[:, b * rank : (b + 1) * rank] for b in range(folds)], axis=0
        )
        slot = block[first, :rows].astype(jnp.float32)
        spread = jnp.where(
            slot[:, None] == columns, jnp.tile(lowered, (1, n * tall // rank)), jnp.bfloat16(0)
        )
        up = jnp.concatenate(ups, axis=0)
        delta = jnp.dot(spread, up, preferred_element_type=jnp.float32).astype(jnp.bfloat16)
        base = sum(b.astype(jnp.float32) for b in bases)
        attended = own_attention(base[rows : rows + dec], *cached)
        base = base[:rows]
        projected = (base + adapter_scale * delta.astype(jnp.float32)).astype(jnp.bfloat16)
        return projected, jnp.concatenate(attended, axis=1)
    cut = 256
    below = bases[0].shape[0] - rows

    def kernel(*refs):
        packs = refs[:4]
        blk, col = refs[4:6]
        bas, upr = refs[6:10], refs[10 : 10 + n]
        own, old = refs[10 + n : 14 + n], refs[14 + n : 18 + n]
        out, out_attended, wide = refs[18 + n :]

        @pl.when(pl.program_id(0) == 0)
        def _():
            slot = jnp.transpose(blk[...].astype(jnp.float32))
            slot = slot[:, first - base_row : first - base_row + 1]
            packed = (packs[0][...] + packs[1][...]) + (packs[2][...] + packs[3][...])
            lane = lax.broadcasted_iota(jnp.int32, packed.shape, 1) // rank
            spread = []
            for b in range(folds):
                one = jnp.where(lane == b, packed, 0.0)
                one = one + pltpu.roll(one, rank, 1)
                one = one + pltpu.roll(one, 2 * rank, 1)
                spread.append(one)
            lowered = jnp.concatenate(spread, axis=0)
            for i in range(0, n * tall, 128):
                kept = jnp.where(slot == col[0:1, i : i + 128], lowered, 0.0)
                wide[:, i : i + 128] = kept.astype(jnp.bfloat16)
            fresh = own[0][...]
            for b in own[1:]:
                fresh = fresh + b[...].astype(jnp.float32)
            parts_own = own_attention(fresh[:dec], *[c[...] for c in old])
            for h in range(heads):
                out_attended[:, h * HEAD_SIZE : (h + 1) * HEAD_SIZE] = parts_own[h]

        up = jnp.concatenate([u[...] for u in upr], axis=0)
        delta = jnp.dot(wide[...], up, preferred_element_type=jnp.float32)
        base = bas[0][0:rows]
        for b in bas[1:]:
            base = base + b[0:rows].astype(jnp.float32)
        out[...] = (base + adapter_scale * delta.astype(jnp.bfloat16).astype(jnp.float32)).astype(
            jnp.bfloat16
        )

    one = lambda j: (0, 0)
    column = lambda j: (0, j)
    return pl.pallas_call(
        kernel,
        grid=(out_width // cut,),
        in_specs=[pl.BlockSpec(parts[0].shape, one)] * 4
        + [
            pl.BlockSpec((16, rows), lambda j: (base_row // 16, 0)),
            pl.BlockSpec(columns.shape, one),
        ]
        + [pl.BlockSpec((bases[0].shape[0], cut), column)] * 4
        + [pl.BlockSpec((tall, cut), column)] * n
        + [pl.BlockSpec((below, out_width), lambda j: (rows // below, 0))] * 4
        + [pl.BlockSpec(a.shape, one) for a in cached],
        out_specs=[pl.BlockSpec((rows, cut), column), pl.BlockSpec(shape, one)],
        out_shape=[
            jax.ShapeDtypeStruct((rows, out_width), jnp.bfloat16),
            jax.ShapeDtypeStruct(shape, jnp.bfloat16),
        ],
        scratch_shapes=[pltpu.VMEM((rows, n * tall), jnp.bfloat16)],
        compiler_params=pltpu.CompilerParams(vmem_limit_bytes=VMEM),
        cost_estimate=cost(2 * rows * n * tall * out_width, 5 * 2**20),
        name="finish",
    )(*parts, block, columns, *bases, *ups, *bases, *cached)


def body(
    prefill_rows,
    tenant_ids,
    owner_slot,
    decode_rows,
    queries,
    key_store_cache,
    value_store_cache,
    context_len,
    base_weight,
    adapter_down,
    adapter_up,
):
    reps, peers = lax.axis_size("replica"), lax.axis_size("tenant")
    planes = reps * peers // 8
    sides = peers // (2 * planes)
    local_slots, rank, width = adapter_down.shape
    slots_all = local_slots * peers
    rows, dec = prefill_rows.shape[0], decode_rows.shape[0]
    out_width = base_weight.shape[1]
    half_width = out_width // 2
    kk = base_weight.shape[0] // reps
    steps = 2 * planes
    quarter = steps * kk
    pad = 16 - dec % 16
    r, t = lax.axis_index("replica"), lax.axis_index("tenant")
    z, y, c = t // (2 * sides), (t // 2) % sides, t % 2
    q = y * reps + r

    order = list(range(0, planes, 2)) + list(range(1, planes, 2))[::-1]
    after = {order[i]: order[(i + 1) % planes] for i in range(planes)}
    everyone = [(a, b) for a in range(reps) for b in range(peers)]

    def flip(m):
        pairs = []
        for a, b in everyone:
            other = (((b // 2) % sides) * reps + a) ^ m
            to = (b // (2 * sides) * sides + other // reps) * 2 + b % 2
            pairs.append((a * peers + b, (other % reps) * peers + to))
        return pairs

    flips = {m: flip(m) for m in (1, 2, 3)}
    ring = [
        (a * peers + b, a * peers + after[b // (2 * sides)] * 2 * sides + b % (2 * sides))
        for a, b in everyone
    ]
    cores = [(a * peers + b, a * peers + (b ^ 1)) for a, b in everyone]

    def send(value, pairs):
        return lax.ppermute(value, BOTH, pairs)

    place = jnp.where(z % 2 == 0, z // 2, planes - 1 - z // 2)

    def plane_of(k):
        spot = (place - k + planes) % planes
        return jnp.where(spot < planes // 2, 2 * spot, 2 * (planes - 1 - spot) + 1)

    spots = jnp.arange(steps, dtype=jnp.int32)
    spots = plane_of(spots // 2) * 2 + (c ^ (spots % 2))
    ranks = local_slots * rank

    def both(value):
        return [value, send(value, cores)]

    def phase(*values):
        return lax.optimization_barrier(values)

    def paired(near, far):
        return near if far is None else jnp.concatenate([near, far], axis=0)

    bases = [lax.dynamic_slice_in_dim(base_weight, r * kk, kk, axis=0)]
    up = adapter_up.reshape(ranks, out_width)
    here, bases, up = phase(jnp.stack([r, y]), bases, up)
    bases.append(send(bases[0], ring))
    up_far = send(up, flips[reps]) if sides == 2 else None
    y_flips = [0, reps] if sides == 2 else [0]
    downs = split_down(adapter_down.reshape(ranks, width), here, steps, kk, reps, sides, y_flips)
    here, downs = phase(here, downs)
    down_far = send(downs[1], flips[reps]) if sides == 2 else None
    messages = split_columns(
        prefill_rows,
        decode_rows,
        tenant_ids.reshape(1, rows),
        owner_slot,
        here,
        steps,
        kk,
        reps,
        sides,
        pad,
    )
    base_parts = both(bases[0])
    bases, downs, down_far, up, up_far, messages, base_parts = phase(
        bases, downs, down_far, up, up_far, messages, base_parts
    )
    near = [send(messages[m], flips[m]) for m in (1, 2)]
    message = messages[0]

    bases.append(send(bases[-1], ring))
    bases, queries = phase(bases, queries)
    while len(bases) < planes:
        bases.append(send(bases[-1], ring))
    downs = [paired(downs[0], down_far)]
    ups = [paired(up, up_far)]
    for held in bases[1:2]:
        base_parts = base_parts + both(held)

    kv_heads = half_width // HEAD_SIZE
    query_groups = queries.shape[1] // half_width
    positions = key_store_cache.shape[1]
    query_head_rows = queries.reshape(dec, kv_heads, query_groups, HEAD_SIZE)
    stored_keys = key_store_cache.reshape(dec, positions, kv_heads, HEAD_SIZE)
    stored_values = value_store_cache.reshape(dec, positions, kv_heads, HEAD_SIZE)
    scale = 1.0 / math.sqrt(HEAD_SIZE)
    scores = (
        jnp.einsum(
            "bkgd,bckd->bkgc", query_head_rows, stored_keys, preferred_element_type=jnp.float32
        )
        * scale
    )
    live = jnp.arange(positions, dtype=jnp.int32)[None, :] < context_len[:, None]
    scores = jnp.where(live[:, None, None, :], scores, -jnp.inf)
    cached_top = jnp.max(scores, axis=-1)
    cached_weight = jnp.exp(scores - cached_top[..., None])
    cached_total = jnp.sum(cached_weight, axis=-1)
    cached_mix = jnp.einsum(
        "bkgc,bckd->bkgd",
        cached_weight.astype(jnp.bfloat16),
        stored_values,
        preferred_element_type=jnp.float32,
    )
    tall = kv_heads * query_groups * dec

    def by_head(value):
        value = value if value.ndim == 4 else value[..., None]
        return value.transpose(1, 2, 0, 3).reshape(tall, value.shape[3])

    cached = [by_head(v) for v in (query_head_rows, cached_top, cached_total, cached_mix)]

    group = jnp.arange(slots_all, dtype=jnp.int32)
    inner = group % local_slots
    side = (group // local_slots) % sides
    core = (group // (local_slots * sides)) % 2
    step = group // (local_slots * sides * 2)
    column_slot = ((plane_of(step) * sides + (y ^ side)) * 2 + (c ^ core)) * local_slots + inner
    columns = jnp.repeat(column_slot, rank).astype(jnp.float32)[None, :]
    core = group // (local_slots * sides * planes)
    step = (group // (local_slots * sides)) % planes
    column_slot = ((plane_of(step) * sides + (y ^ side)) * 2 + (c ^ core)) * local_slots + inner
    up_columns = jnp.repeat(column_slot, rank).astype(jnp.float32)[None, :]

    pieces = both(downs[0])
    near, bases, ups, far, base_parts, pieces, cached, columns, up_columns, spots = phase(
        near, bases, ups, messages[3], base_parts, pieces, cached, columns, up_columns, spots
    )

    far = send(far, flips[3])
    while len(downs) < max(2, planes - 1):
        downs.append(send(downs[-1], ring))
    for held in bases[2:]:
        base_parts = base_parts + both(held)
    partials = base_products(near, base_parts, spots, [jnp.bfloat16] * 2)
    up_cores = [send(ups[0], cores)]
    pieces = pieces + both(downs[1])
    far, downs, ups, partials, base_parts, up_cores, pieces = phase(
        far, downs, ups, partials, base_parts, up_cores, pieces
    )

    base = [send(partials[m - 1], flips[m]) for m in (1, 2)]
    while len(downs) < planes:
        downs.append(send(downs[-1], ring))
    ups.append(send(ups[0], ring))
    last, own = base_products([far, message], base_parts, spots, [jnp.bfloat16, jnp.float32])
    pieces = pieces + sum([both(d) for d in downs[2:-1]], [])
    base, downs, ups, last, own, pieces, up_cores = phase(
        base, downs, ups, last, own, pieces, up_cores
    )

    base = [own, *base, send(last, flips[3])]
    blocks = [message, *near, far]
    pieces = pieces + both(downs[-1])
    for k in range(2, planes):
        after_k = {order[i]: order[(i + k) % planes] for i in range(planes)}
        pairs = []
        for a, b in everyone:
            to = after_k[b // (2 * sides)] * 2 * sides + b % (2 * sides)
            pairs.append((a * peers + b, a * peers + to))
        ups.append(send(ups[0], pairs))
    first = rows + dec
    packed = lowered_products(blocks, pieces, columns, rows, first, rank, last)
    packed = [packed[0]] + [send(packed[m], flips[m]) for m in (1, 2, 3)]
    packed, ups = phase(packed, ups)
    up_parts = ups + up_cores + [send(u, cores) for u in ups[1:]]
    base, packed, up_parts = phase(base, packed, up_parts)
    return tuple(
        finish(
            packed,
            message,
            up_parts,
            up_columns,
            base,
            rows,
            first,
            rank,
            cached,
            dec,
        )
    )


def solution(mesh):
    in_specs = (
        P(BOTH, None),
        P(BOTH, None),
        P(),
        P(BOTH, None),
        P(BOTH, None),
        P(BOTH, None, None),
        P(BOTH, None, None),
        P(BOTH),
        P("tenant", None),
        P("tenant", None, None),
        P("tenant", None, None),
    )
    out_specs = (P(BOTH, None), P(BOTH, None))
    return jax.shard_map(body, mesh=mesh, in_specs=in_specs, out_specs=out_specs, check_vma=False)
```
